32 devices in a mesh: groups: 2 (over x), src: 16 (over z, y, core).
Axes of the slice: x: 2, y: 2, z: 4, core: 2. Of those that a mesh axis runs over, the one named last changes fastest.
Arguments:
- layout_mask: int32 [512, 256], P('groups'), parts along dimension 0, may hold values 0 or 1
- source_coords: int32 [32, 2], P('src'), may hold values from -8 to 8
- source_weights: int32 [32], P('src'), may hold values from 1 to 8
- focus_steps: int32 [16], replicated, may hold values from -4 to 4
- pupil_taps: float32 [48], replicated, may hold values from 0.25 to 1.75
- blur_x: float32 [31], replicated, may hold values from 0 to 2
- blur_y: float32 [31], replicated, may hold values from 0 to 2
- blur_z: float32 [31], replicated, may hold values from 0 to 2
Outputs:
- intensity: float32 [8192, 256], P(('groups', 'src')), parts along dimension 0
- latent: float32 [8192, 256], P(('groups', 'src')), parts along dimension 0
The draws below stay inside these ranges and needn't reach their ends.
There are 2 independent parts, one for each index of `groups`. The reference program is written for one: setup_inputs(seed, part) draws one part's arguments, and reference() takes and returns one part's arrays. A program takes and returns all parts, laid end to end along the dimension named above; an argument that names none is the same for every part. Nothing has to cross between parts.
All inputs are finite; a program needn't handle non-finite values.
Results may differ from the reference program's by a relative error of at most 0.0022.
Values sent between devices are 32-bit elements; how exact they have to be, the bound alone decides.
A program may use at most 64 MiB of HBM per device.

```python
import math
import jax
import jax.numpy as jnp
from jax import lax

H = 256
W = 256
F = 16
PT = 48
HB = 15
S = 32


def set_ends(drawn, rng, least, high):
    longest = drawn.shape.index(max(drawn.shape))
    spots = []
    for shift in (0, 1):
        where = [jax.random.randint(jax.random.fold_in(rng, axis), (), 0, length) for axis, length in enumerate(drawn.shape)]
        where[longest] = (where[longest] + shift) % drawn.shape[longest]
        spots.append(tuple(where))
    return drawn.at[spots[0]].set(least).at[spots[1]].set(high)


def setup_inputs(seed: int = 0, part: int = 0) -> dict:
    splits = jax.random.split(jax.random.key(seed), 9)
    part_splits = jax.random.split(jax.random.fold_in(splits[8], part), 9)
    layout_mask = set_ends((jax.random.randint(part_splits[0], (H, W), 0, 5) < 2).astype(jnp.int32), jax.random.fold_in(part_splits[0], 1), 0, 1)
    source_coords = set_ends(jax.random.randint(splits[1], (S, 2), -8, 9), jax.random.fold_in(splits[1], 1), -8, 8).astype(jnp.int32)
    source_weights = set_ends(jax.random.randint(splits[2], (S,), 1, 9), jax.random.fold_in(splits[2], 1), 1, 8).astype(jnp.int32)
    focus_steps = set_ends(jax.random.randint(splits[3], (F,), -4, 5), jax.random.fold_in(splits[3], 1), -4, 4).astype(jnp.int32)
    pupil_taps = jnp.clip(1.0 + 0.15 * jax.random.normal(splits[4], (PT,), jnp.float32), 0.25, 1.75)
    blur_x = jnp.clip(jax.random.uniform(splits[5], (2 * HB + 1,), jnp.float32, 0.0, 2.0), 0.0, 2.0)
    blur_y = jnp.clip(jax.random.uniform(splits[6], (2 * HB + 1,), jnp.float32, 0.0, 2.0), 0.0, 2.0)
    blur_z = jnp.clip(jax.random.uniform(splits[7], (2 * F - 1,), jnp.float32, 0.0, 2.0), 0.0, 2.0)
    return {"layout_mask": layout_mask, "source_coords": source_coords, "source_weights": source_weights, "focus_steps": focus_steps, "pupil_taps": pupil_taps, "blur_x": blur_x, "blur_y": blur_y, "blur_z": blur_z}


two_pi = 2.0 * math.pi
defocus_scale = 0.8
dose_scale = 2.0

def to_wide(values):
    return lax.optimization_barrier(values.astype(jnp.bfloat16)).astype(jnp.float32)

def tap_matrix(out_pos, extent, tilt_index, focus_step, pupil_taps):
    tap_count = pupil_taps.shape[0]
    centre = (tap_count - 1) / 2.0
    column_pos = jnp.arange(extent, dtype=jnp.int32)
    offset = column_pos[None, :] - out_pos[:, None] + tap_count // 2
    inside = (offset >= 0) & (offset < tap_count)
    clipped = jnp.clip(offset, 0, tap_count - 1).astype(jnp.int32)
    amplitude = jnp.take(pupil_taps, clipped) / math.sqrt(tap_count)
    relative = clipped.astype(jnp.float32) - centre
    phase_angle = two_pi * tilt_index.astype(jnp.float32) * relative / tap_count + defocus_scale * focus_step.astype(jnp.float32) * (relative / centre) ** 2
    real_part = jnp.where(inside, amplitude * jnp.cos(phase_angle), jnp.zeros_like(amplitude))
    imag_part = jnp.where(inside, amplitude * jnp.sin(phase_angle), jnp.zeros_like(amplitude))
    return (to_wide(real_part), to_wide(imag_part))

def field_power(mask_wide, tilt_x, tilt_y, focus_step, pupil_taps):
    rows_tile, cols_tile = mask_wide.shape
    row_pos = jnp.arange(rows_tile, dtype=jnp.int32)
    col_pos = jnp.arange(cols_tile, dtype=jnp.int32)
    rows_real, rows_imag = tap_matrix(row_pos, rows_tile, tilt_y, focus_step, pupil_taps)
    cols_real, cols_imag = tap_matrix(col_pos, cols_tile, tilt_x, focus_step, pupil_taps)
    stacked = jnp.concatenate([rows_real, rows_imag], axis=0)
    first_pass = to_wide(jnp.dot(stacked, mask_wide, precision=lax.Precision.HIGHEST))
    joined = jnp.concatenate([first_pass[:rows_tile], first_pass[rows_tile:]], axis=1)
    upper_half = jnp.concatenate([cols_real.T, cols_imag.T], axis=1)
    lower_half = jnp.concatenate([-cols_imag.T, cols_real.T], axis=1)
    pupil_cols = jnp.concatenate([upper_half, lower_half], axis=0)
    field_parts = jnp.dot(joined, pupil_cols, precision=lax.Precision.HIGHEST)
    return field_parts[:, :cols_tile] ** 2 + field_parts[:, cols_tile:] ** 2

def reference(layout_mask, source_coords, source_weights, focus_steps, pupil_taps, blur_x, blur_y, blur_z):
    rows_tile, cols_tile = layout_mask.shape
    planes = focus_steps.shape[0]
    total_src = source_coords.shape[0]
    mask_wide = layout_mask.astype(jnp.float32)
    factors = source_weights.astype(jnp.float32) / (4.0 * total_src)

    def add_source(running, source_item):
        point_coords, weight_factor = source_item

        def one_plane(focus_step):
            return field_power(mask_wide, point_coords[0], point_coords[1], focus_step, pupil_taps)
        powers = lax.map(one_plane, focus_steps)
        return (running + weight_factor * powers, None)
    start_stack = jnp.zeros((planes, rows_tile, cols_tile), jnp.float32)
    intensity_stack = lax.scan(add_source, start_stack, (source_coords, factors))[0]
    intensity = intensity_stack.reshape(planes * rows_tile, cols_tile)
    acid_level = 1.0 - jnp.exp(-dose_scale * intensity)
    width_x = blur_x.shape[0]
    half_x = width_x // 2
    padded = jnp.pad(acid_level, ((0, 0), (half_x, half_x)))
    along_x = jnp.zeros_like(acid_level)
    for tap_index in range(width_x):
        along_x = along_x + blur_x[tap_index] / width_x * padded[:, tap_index:tap_index + cols_tile]
    width_y = blur_y.shape[0]
    half_y = width_y // 2
    total_rows = planes * rows_tile
    padded = jnp.pad(along_x, ((half_y, half_y), (0, 0)))
    along_y = jnp.zeros_like(along_x)
    for tap_index in range(width_y):
        along_y = along_y + blur_y[tap_index] / width_y * padded[tap_index:tap_index + total_rows, :]
    along_y = along_y.reshape(planes, rows_tile, cols_tile)
    plane_pos = jnp.arange(planes, dtype=jnp.int32)
    lag_index = (plane_pos[:, None] - plane_pos[None, :] + planes - 1).astype(jnp.int32)
    focus_matrix = jnp.take(blur_z, lag_index) / planes
    latent = jnp.einsum('pq,qyx->pyx', focus_matrix, along_y, precision=lax.Precision.HIGHEST)
    return (intensity, latent.reshape(planes * rows_tile, cols_tile))
```

```python
import math

import jax
import jax.numpy as jnp
from jax import lax
from jax.experimental import pallas as pl
from jax.experimental.pallas import tpu as pltpu
from jax.sharding import PartitionSpec as P

two_pi = 2.0 * math.pi
defocus_scale = 0.8
dose_scale = 2.0


def extended_2(block, sides, width):
    for axis, dim in sides:
        count = lax.axis_size(axis)
        forward = [(i, i + 1) for i in range(count - 1)]
        backward = [(target, source) for source, target in forward]
        low = lax.ppermute(
            lax.slice_in_dim(block, block.shape[dim] - width, None, axis=dim), axis, forward
        )
        high = lax.ppermute(lax.slice_in_dim(block, 0, width, axis=dim), axis, backward)
        block = jnp.concatenate([low, block, high], axis=dim)
    return block


def passed_along(block, axis, distance):
    devices = range(lax.axis_size(axis))
    route = [(i - distance, i) for i in devices if i - distance in devices]
    return lax.ppermute(block, axis, route)


def tap_matrix(out_pos, extent, tilt_index, focus_step, pupil_taps):
    tap_count = pupil_taps.shape[0]
    centre = (tap_count - 1) / 2.0
    column_pos = jnp.arange(extent, dtype=jnp.int32)
    offset = column_pos[None, :] - out_pos[:, None] + tap_count // 2
    inside = (offset >= 0) & (offset < tap_count)
    clipped = jnp.clip(offset, 0, tap_count - 1)
    amplitude = jnp.take(pupil_taps, clipped) / math.sqrt(tap_count)
    relative = clipped.astype(jnp.float32) - centre
    phase_angle = (
        two_pi * tilt_index.astype(jnp.float32) * relative / tap_count
        + defocus_scale * focus_step.astype(jnp.float32) * (relative / centre) ** 2
    )
    real_part = jnp.where(inside, amplitude * jnp.cos(phase_angle), jnp.zeros_like(amplitude))
    imag_part = jnp.where(inside, amplitude * jnp.sin(phase_angle), jnp.zeros_like(amplitude))
    return (real_part.astype(jnp.bfloat16), imag_part.astype(jnp.bfloat16))


def field_power(mask_bf, row_pos, tilt_x, tilt_y, focus_step, pupil_taps):
    rows_tile, cols_tile = mask_bf.shape
    row_count = row_pos.shape[0]
    col_pos = jnp.arange(cols_tile, dtype=jnp.int32)
    rows_real, rows_imag = tap_matrix(row_pos, rows_tile, tilt_y, focus_step, pupil_taps)
    cols_real, cols_imag = tap_matrix(col_pos, cols_tile, tilt_x, focus_step, pupil_taps)
    stacked = jnp.concatenate([rows_real, rows_imag], axis=0)
    first_pass = jnp.dot(stacked, mask_bf, preferred_element_type=jnp.float32).astype(jnp.bfloat16)
    joined = jnp.concatenate([first_pass[:row_count], first_pass[row_count:]], axis=1)
    upper_half = jnp.concatenate([cols_real.T, cols_imag.T], axis=1)
    lower_half = jnp.concatenate([-cols_imag.T, cols_real.T], axis=1)
    pupil_cols = jnp.concatenate([upper_half, lower_half], axis=0)
    field_parts = jnp.dot(joined, pupil_cols, preferred_element_type=jnp.float32)
    return field_parts[:, :cols_tile] ** 2 + field_parts[:, cols_tile:] ** 2


def on_device(
    layout_mask, source_coords, source_weights, focus_steps, pupil_taps, blur_x, blur_y, blur_z
):
    rows_tile, cols_tile = layout_mask.shape
    planes = focus_steps.shape[0]
    devices = lax.axis_size("src")
    src_local = source_coords.shape[0]
    mask_bf = layout_mask.astype(jnp.bfloat16)
    own_rows = planes * rows_tile // devices
    per_plane = devices // planes
    factors = source_weights.astype(jnp.float32) / (4.0 * src_local * devices)
    row_pos = jnp.arange(rows_tile, dtype=jnp.int32)

    def plane_term(focus_step):
        running = jnp.zeros((rows_tile, cols_tile), jnp.float32)
        for source in range(src_local):
            power = field_power(
                mask_bf,
                row_pos,
                source_coords[source, 0],
                source_coords[source, 1],
                focus_step,
                pupil_taps,
            )
            running = running + factors[source] * power
        return running

    partial_sum = lax.map(plane_term, focus_steps).reshape(planes * rows_tile, cols_tile)
    intensity = lax.psum_scatter(partial_sum, "src", scatter_dimension=0, tiled=True)
    acid_level = 1.0 - jnp.exp(-dose_scale * intensity)
    width_x = blur_x.shape[0]
    half_x = width_x // 2
    padded = jnp.pad(acid_level, ((0, 0), (half_x, half_x)))
    along_x = jnp.zeros_like(acid_level)
    for tap_index in range(width_x):
        along_x = (
            along_x + blur_x[tap_index] / width_x * padded[:, tap_index : tap_index + cols_tile]
        )
    width_y = blur_y.shape[0]
    half_y = width_y // 2
    extended = extended_2(along_x, (("src", 0),), half_y)
    along_y = jnp.zeros_like(along_x)
    for tap_index in range(width_y):
        along_y = along_y + blur_y[tap_index] / width_y * extended[tap_index : tap_index + own_rows]
    latent = blur_z[planes - 1] / planes * along_y
    for plane_lag in range(1 - planes, planes):
        if plane_lag != 0:
            arrived = passed_along(along_y, "src", plane_lag * per_plane)
            latent = latent + blur_z[plane_lag + planes - 1] / planes * arrived
    return (intensity, latent)


max_shift = 8
shifts = 2 * max_shift + 1
lanes = 512
devices_unrolled = 16


def exact_dot(left, right):
    def halves(value):
        high = value.astype(jnp.bfloat16)
        return high, (value - high.astype(jnp.float32)).astype(jnp.bfloat16)

    def product(a, b):
        return jnp.dot(a, b, preferred_element_type=jnp.float32)

    left_high, left_low = halves(left)
    right_high, right_low = halves(right)
    return (
        product(left_high, right_low) + product(left_low, right_high)
    ) + product(left_high, right_high)


def store_toeplitz(row, position, pieces, apart=128):
    base = pltpu.roll(jnp.broadcast_to(row, (16, 128)), 0, 1, stride=1, stride_axis=0)
    lane = lax.broadcasted_iota(jnp.int32, (16, 128), 1)
    zero = jnp.zeros((16, 128), jnp.float32)
    for j in range(8):
        first = 16 * j + position - 256
        turn, tile = first % 128, first // 128
        rolled = pltpu.roll(base, turn, 1) if turn else base
        wraps = turn > 65
        kept = jnp.where(lane >= turn, rolled, zero) if wraps else rolled
        wrapped = jnp.where(lane < turn, rolled, zero) if wraps else zero
        for block, start in ((j, tile), (j + 8, tile + 1)):
            for column in range(2):
                part = kept if column == start else wrapped if column == start + 1 else zero
                for ref, top, side, sign in pieces:
                    value = part if sign > 0 else -part
                    left = side + apart * column
                    ref[top + 16 * block : top + 16 * block + 16, left : left + 128] = (
                        value.astype(ref.dtype)
                    )


def store_taps(taps_ref, row, focus, flip, real_ref, imag_ref, tap_count):
    centre = (tap_count - 1) / 2.0
    amplitude = taps_ref[row : row + 1, :128] / math.sqrt(tap_count)
    shape = (24, 128)
    relative = (lax.broadcasted_iota(jnp.int32, shape, 1).astype(jnp.float32) - centre) * flip
    tilt = (lax.broadcasted_iota(jnp.int32, shape, 0) - max_shift).astype(jnp.float32)
    phase = (
        two_pi * tilt * relative / tap_count + defocus_scale * focus * (relative / centre) ** 2
    )
    real_ref[...] = amplitude * jnp.cos(phase)
    imag_ref[...] = amplitude * jnp.sin(phase)


def toeplitz_tiles(row, position, blocks):
    base = pltpu.roll(jnp.broadcast_to(row, (16, 128)), 0, 1, stride=1, stride_axis=0)
    apart = lax.broadcasted_iota(jnp.int32, (16, 128), 1) - lax.broadcasted_iota(
        jnp.int32, (16, 128), 0
    )
    tiles = {}
    for block in blocks:
        turn = 16 * block - position
        tile = pltpu.roll(base, turn % 128, 1) if turn % 128 else base
        if 127 - turn >= 128:
            tile = jnp.where(apart < 128 + turn, tile, 0.0)
        if -15 - turn < -80:
            tile = jnp.where(apart >= turn - 80, tile, 0.0)
        tiles[block] = tile
    return tiles


def build_columns(forward_real, forward_imag, shapes):
    def one_shift(shift):
        row = pl.ds(shift, 1)
        real = toeplitz_tiles(forward_real[row, :], 24, range(8))
        imag = toeplitz_tiles(forward_imag[row, :], 24, range(8))
        for j in range(8):
            re, im = real[j].astype(jnp.bfloat16), imag[j].astype(jnp.bfloat16)
            upper, lower = slice(16 * j, 16 * j + 16), slice(128 + 16 * j, 144 + 16 * j)
            shapes[shift, upper, :128] = re
            shapes[shift, upper, 128:] = -im
            shapes[shift, lower, :128] = im
            shapes[shift, lower, 128:] = re

    def four_shifts(step, carry):
        for place in range(4):
            one_shift(4 * step + place)
        return carry

    lax.fori_loop(0, shifts // 4, four_shifts, 0)
    one_shift(shifts - 1)


def build_fields(back_real, back_imag, mask_ref, slots, fields):
    mask_turned = mask_ref[...].astype(jnp.float32).T.astype(jnp.bfloat16)

    def one_shift(shift, slot):
        row = pl.ds(shift, 1)
        for side, source in ((0, back_real), (256, back_imag)):
            tiles = toeplitz_tiles(source[row, :], 23, range(-2, 10))
            for block, tile in tiles.items():
                value = tile.astype(jnp.bfloat16)
                if block >= 0:
                    slots[slot, 16 * block : 16 * block + 16, side : side + 128] = value
                if block < 8:
                    top = 16 * block + 128
                    slots[slot, top : top + 16, side + 128 : side + 256] = value
        fields[shift] = jnp.dot(
            mask_turned, slots[slot], preferred_element_type=jnp.float32
        ).astype(jnp.bfloat16)

    def four_shifts(step, carry):
        for slot in range(4):
            one_shift(4 * step + slot, slot)
        return carry

    lax.fori_loop(0, shifts // 4, four_shifts, 0)
    one_shift(shifts - 1, 0)


def lane_row(count, value):
    lane = lax.broadcasted_iota(jnp.int32, (1, lanes), 1)
    row = jnp.zeros((1, lanes), jnp.float32)
    for t in range(count):
        row = jnp.where(lane == t, value(t), row)
    return row


def plane_kernel(
    n, wide, mask_hbm, coords_hbm, weights_hbm, focus_hbm, taps_hbm, blur_x_hbm, blur_y_hbm,
    blur_z_hbm, intensity_ref, latent_ref, mask_ref, coords_ref, weights_ref, focus_ref, taps_ref,
    blur_x_ref, blur_y_ref, blur_z_ref, arg_sems, rows, t0, t1, t2, t3, slots, fields, shapes, image,
    acid, centre, mix, own, points, points_smem, along, columns, mixed, planes, send_sems, recv_sems,
    local_sem,
):
    me = lax.axis_index("src")
    group = lax.axis_index("groups")
    local = weights_ref.shape[0]
    tap_count, blur_count = taps_ref.shape[0], blur_x_ref.shape[0]
    barrier = pltpu.get_barrier_semaphore()

    def each(action):
        lax.fori_loop(1, n, lambda off, carry: (action(off), carry)[1], 0)

    def peer(off):
        return (group, lax.rem(me + off, n))

    def signal(off):
        pl.semaphore_signal(
            barrier, inc=1, device_id=peer(off), device_id_type=pl.DeviceIdType.MESH
        )

    def copy(phase, source, target, off, slot):
        return pltpu.make_async_remote_copy(
            src_ref=source(off),
            dst_ref=target.at[slot],
            send_sem=send_sems.at[phase, off],
            recv_sem=recv_sems.at[phase, off],
            device_id=peer(off),
            device_id_type=pl.DeviceIdType.MESH,
        )

    def start(phase, source, target):
        each(lambda off: copy(phase, source, target, off, me).start())

    def receive(phase, source, target):
        each(
            lambda off: copy(phase, source, target, off, lax.rem(me + n - off, n)).wait_recv()
        )

    def sent(phase, source, target):
        each(lambda off: copy(phase, source, target, off, me).wait_send())

    def blocks(ref, part):
        return lambda off: ref.at[part, lax.rem(me + off, n)]

    fetches = [
        pltpu.make_async_copy(source, target, arg_sems.at[place])
        for place, (source, target) in enumerate(
            (
                (coords_hbm, coords_ref),
                (weights_hbm, weights_ref),
                (focus_hbm, focus_ref),
                (taps_hbm, taps_ref),
                (blur_x_hbm, blur_x_ref),
                (blur_y_hbm, blur_y_ref),
                (blur_z_hbm, blur_z_ref),
                (mask_hbm, mask_ref),
            )
        )
    ]
    for fetch in fetches:
        fetch.start()
    each(signal)
    slots[...] = jnp.zeros_like(slots)
    for fetch in fetches:
        fetch.wait()
    lane = lax.broadcasted_iota(jnp.int32, (1, 128), 1)
    packed = jnp.zeros((1, 128), jnp.int32)
    for s in range(local):
        packed = jnp.where(lane == 3 * s, coords_ref[s, 0], packed)
        packed = jnp.where(lane == 3 * s + 1, coords_ref[s, 1], packed)
        packed = jnp.where(lane == 3 * s + 2, weights_ref[s], packed)
    own[...] = packed
    points[me] = packed
    rows[0:1, :] = lane_row(tap_count, lambda t: taps_ref[t])
    rows[1:2, :] = lane_row(tap_count, lambda t: taps_ref[tap_count - 1 - t])
    rows[2:3, :] = lane_row(blur_count, lambda t: blur_x_ref[t] / blur_count)
    rows[3:4, :] = lane_row(blur_count, lambda t: blur_y_ref[blur_count - 1 - t] / blur_count)
    focus = focus_ref[me].astype(jnp.float32)
    store_taps(rows, 0, focus, 1.0, t0, t1, tap_count)
    store_taps(rows, 1, focus, -1.0, t2, t3, tap_count)
    build_columns(t0, t1, shapes)
    pl.semaphore_wait(barrier, n - 1)
    point_source = lambda off: own
    start(0, point_source, points)
    build_fields(t2, t3, mask_ref, slots, fields)
    image[...] = jnp.zeros_like(image)
    tiles = toeplitz_tiles(rows[2:3, :128], 15, range(-1, 9))
    blank = jnp.zeros((96, 128), jnp.float32)
    blur_first = jnp.concatenate([tiles[j] for j in range(4)], axis=0)[:, :96]
    blur_last = jnp.concatenate([tiles[j] for j in range(2, 6)], axis=0)[:, :96]
    blur_middle = jnp.concatenate(
        [
            jnp.concatenate([tiles[j] for j in range(1, 9)], axis=0),
            jnp.concatenate([blank, tiles[-1], tiles[0]], axis=0)[:, :32],
        ],
        axis=1,
    )
    back_y = rows[3:4, :]
    store_toeplitz(rows[3:4, :128], 241, ((centre, 0, 0, 1),))
    tall = jnp.broadcast_to(back_y, (16, lanes))
    before = pltpu.roll(tall, lanes - 31, 1, stride=1, stride_axis=0)[:, :256]
    after = pltpu.roll(tall, 241, 1, stride=1, stride_axis=0)[:, :256]
    pad = jnp.zeros((112, 256), jnp.float32)
    size = n * wide
    distance = lax.broadcasted_iota(jnp.int32, (size, size), 0) - lax.broadcasted_iota(
        jnp.int32, (size, size), 1
    )
    mixing = jnp.zeros((size, size), jnp.float32)
    for lag in range(1 - n, n):
        mixing = jnp.where(distance == lag * wide, blur_z_ref[lag + n - 1] / n, mixing)
    mix[...] = mixing
    receive(0, point_source, points)
    to_smem = pltpu.make_async_copy(points, points_smem, local_sem)
    to_smem.start()
    to_smem.wait()

    def image_columns(left, low, high, first):
        count = high - low

        def some_devices(step, carry):
            power = jnp.zeros((count, 256), jnp.float32)
            for place in range(devices_unrolled * local):
                device, s = devices_unrolled * step + place // local, place % local
                point = [points_smem[device, 0, 3 * s + item] for item in range(3)]
                factor = point[2].astype(jnp.float32) / (4.0 * local * n)
                column, row = point[0] + max_shift, point[1] + max_shift
                field = jnp.dot(
                    jnp.concatenate(
                        [shapes[column, low:high], shapes[column, 128 + low : 128 + high]], axis=0
                    ),
                    jnp.concatenate(
                        [
                            fields[row, first : first + 128, :256],
                            fields[row, first : first + 128, 256:],
                        ],
                        axis=0,
                    ),
                    preferred_element_type=jnp.float32,
                )
                power = power + factor * (field[:count] ** 2 + field[count:] ** 2)
            image[left : left + count] += power
            return carry

        lax.fori_loop(0, n // devices_unrolled, some_devices, 0)
        acid[left : left + count] = 1.0 - jnp.exp(-dose_scale * image[left : left + count])

    def send_columns(part, values):
        along[part] = values.reshape(n, wide, 256)
        start(1 + part, blocks(along, part), columns.at[part])
        columns[part, me] = along[part, me]

    def mix_planes(part):
        receive(1 + part, blocks(along, part), columns.at[part])
        stack = columns[part].reshape(size, 256)
        zero = jnp.zeros((wide, 128), jnp.float32)
        along_y = (
            exact_dot(stack, centre[...])
            + exact_dot(
                jnp.concatenate([zero, stack[:-wide, 128:]], axis=0),
                jnp.concatenate([pad, before], axis=0),
            )
            + exact_dot(
                jnp.concatenate([stack[wide:, :128], zero], axis=0),
                jnp.concatenate([after, pad], axis=0),
            )
        )
        mixed[part] = exact_dot(mix[...], along_y).reshape(n, wide, 256)
        start(3 + part, blocks(mixed, part), planes.at[part])
        planes[part, me] = mixed[part, me]

    image_columns(0, 0, 96, 0)
    image_columns(160, 32, 128, 128)
    send_columns(
        0,
        jnp.concatenate(
            [exact_dot(blur_first, acid[:96]), exact_dot(blur_last, acid[160:])], axis=0
        ),
    )
    image_columns(96, 32, 96, 64)
    send_columns(1, exact_dot(blur_middle, acid[48:208]))
    intensity_ref[...] = image[...].T
    mix_planes(0)
    mix_planes(1)
    sent(0, point_source, points)
    receive(3, blocks(mixed, 0), planes.at[0])
    outer = planes[0].reshape(size, 256)
    latent_ref[:, :64] = outer[:64].T
    latent_ref[:, 192:] = outer[64:].T
    receive(4, blocks(mixed, 1), planes.at[1])
    latent_ref[:, 64:192] = planes[1].reshape(size, 256).T
    for part in range(2):
        sent(1 + part, blocks(along, part), columns.at[part])
        sent(3 + part, blocks(mixed, part), planes.at[part])


def plane_per_device(
    layout_mask, source_coords, source_weights, focus_steps, pupil_taps, blur_x, blur_y, blur_z
):
    n = lax.axis_size("src")
    wide = layout_mask.shape[1] // n // 2
    square = jax.ShapeDtypeStruct((256, 256), jnp.float32)
    full = pltpu.VMEM((256, 256), jnp.float32)
    parts = pltpu.VMEM((2, n, wide, 256), jnp.float32)
    vmem = pl.BlockSpec(memory_space=pltpu.VMEM)
    hbm = pl.BlockSpec(memory_space=pltpu.HBM)
    arguments = (
        source_coords, source_weights, focus_steps, pupil_taps, blur_x, blur_y, blur_z
    )
    return pl.pallas_call(
        lambda *refs: plane_kernel(n, wide, *refs),
        out_shape=(square, square),
        in_specs=[hbm] * 8,
        out_specs=(vmem, vmem),
        scratch_shapes=[pltpu.VMEM((256, 256), jnp.int32)]
        + [pltpu.SMEM(value.shape, value.dtype) for value in arguments]
        + [pltpu.SemaphoreType.DMA((8,)), pltpu.VMEM((8, lanes), jnp.float32)]
        + [pltpu.VMEM((24, 128), jnp.float32)] * 4
        + [
            pltpu.VMEM((4, 256, 512), jnp.bfloat16),
            pltpu.VMEM((shifts, 256, 512), jnp.bfloat16),
            pltpu.VMEM((shifts, 256, 256), jnp.bfloat16),
            full,
            full,
            full,
            pltpu.VMEM((n * wide, n * wide), jnp.float32),
            pltpu.VMEM((1, 128), jnp.int32),
            pltpu.VMEM((n, 1, 128), jnp.int32),
            pltpu.SMEM((n, 1, 128), jnp.int32),
            parts,
            parts,
            parts,
            parts,
            pltpu.SemaphoreType.DMA((5, n)),
            pltpu.SemaphoreType.DMA((5, n)),
            pltpu.SemaphoreType.DMA,
        ],
        compiler_params=pltpu.CompilerParams(
            vmem_limit_bytes=64 * 2**20 - 2**17, collective_id=0, has_side_effects=True
        ),
    )(layout_mask, *arguments)


def solution(mesh):
    in_specs = (P("groups", None), P("src", None), P("src"), P(), P(), P(), P(), P())
    out_specs = (P(("groups", "src"), None), P(("groups", "src"), None))
    body = plane_per_device if mesh.shape["src"] == 16 else on_device
    return jax.shard_map(
        body, mesh=mesh, in_specs=in_specs, out_specs=out_specs, check_vma=False
    )
```

```python
import math

import jax
import jax.numpy as jnp
from jax import lax
from jax.experimental import pallas as pl
from jax.experimental.pallas import tpu as pltpu
from jax.sharding import PartitionSpec as P

two_pi = 2.0 * math.pi
defocus_scale = 0.8
dose_scale = 2.0


def extended_2(block, sides, width):
    for axis, dim in sides:
        count = lax.axis_size(axis)
        forward = [(i, i + 1) for i in range(count - 1)]
        backward = [(target, source) for source, target in forward]
        low = lax.ppermute(
            lax.slice_in_dim(block, block.shape[dim] - width, None, axis=dim), axis, forward
        )
        high = lax.ppermute(lax.slice_in_dim(block, 0, width, axis=dim), axis, backward)
        block = jnp.concatenate([low, block, high], axis=dim)
    return block


def passed_along(block, axis, distance):
    devices = range(lax.axis_size(axis))
    route = [(i - distance, i) for i in devices if i - distance in devices]
    return lax.ppermute(block, axis, route)


def tap_matrix(out_pos, extent, tilt_index, focus_step, pupil_taps):
    tap_count = pupil_taps.shape[0]
    centre = (tap_count - 1) / 2.0
    column_pos = jnp.arange(extent, dtype=jnp.int32)
    offset = column_pos[None, :] - out_pos[:, None] + tap_count // 2
    inside = (offset >= 0) & (offset < tap_count)
    clipped = jnp.clip(offset, 0, tap_count - 1)
    amplitude = jnp.take(pupil_taps, clipped) / math.sqrt(tap_count)
    relative = clipped.astype(jnp.float32) - centre
    phase_angle = (
        two_pi * tilt_index.astype(jnp.float32) * relative / tap_count
        + defocus_scale * focus_step.astype(jnp.float32) * (relative / centre) ** 2
    )
    real_part = jnp.where(inside, amplitude * jnp.cos(phase_angle), jnp.zeros_like(amplitude))
    imag_part = jnp.where(inside, amplitude * jnp.sin(phase_angle), jnp.zeros_like(amplitude))
    return (real_part.astype(jnp.bfloat16), imag_part.astype(jnp.bfloat16))


def field_power(mask_bf, row_pos, tilt_x, tilt_y, focus_step, pupil_taps):
    rows_tile, cols_tile = mask_bf.shape
    row_count = row_pos.shape[0]
    col_pos = jnp.arange(cols_tile, dtype=jnp.int32)
    rows_real, rows_imag = tap_matrix(row_pos, rows_tile, tilt_y, focus_step, pupil_taps)
    cols_real, cols_imag = tap_matrix(col_pos, cols_tile, tilt_x, focus_step, pupil_taps)
    stacked = jnp.concatenate([rows_real, rows_imag], axis=0)
    first_pass = jnp.dot(stacked, mask_bf, preferred_element_type=jnp.float32).astype(jnp.bfloat16)
    joined = jnp.concatenate([first_pass[:row_count], first_pass[row_count:]], axis=1)
    upper_half = jnp.concatenate([cols_real.T, cols_imag.T], axis=1)
    lower_half = jnp.concatenate([-cols_imag.T, cols_real.T], axis=1)
    pupil_cols = jnp.concatenate([upper_half, lower_half], axis=0)
    field_parts = jnp.dot(joined, pupil_cols, preferred_element_type=jnp.float32)
    return field_parts[:, :cols_tile] ** 2 + field_parts[:, cols_tile:] ** 2


def on_device(
    layout_mask, source_coords, source_weights, focus_steps, pupil_taps, blur_x, blur_y, blur_z
):
    rows_tile, cols_tile = layout_mask.shape
    planes = focus_steps.shape[0]
    devices = lax.axis_size("src")
    src_local = source_coords.shape[0]
    mask_bf = layout_mask.astype(jnp.bfloat16)
    own_rows = planes * rows_tile // devices
    per_plane = devices // planes
    factors = source_weights.astype(jnp.float32) / (4.0 * src_local * devices)
    row_pos = jnp.arange(rows_tile, dtype=jnp.int32)

    def plane_term(focus_step):
        running = jnp.zeros((rows_tile, cols_tile), jnp.float32)
        for source in range(src_local):
            power = field_power(
                mask_bf,
                row_pos,
                source_coords[source, 0],
                source_coords[source, 1],
                focus_step,
                pupil_taps,
            )
            running = running + factors[source] * power
        return running

    partial_sum = lax.map(plane_term, focus_steps).reshape(planes * rows_tile, cols_tile)
    intensity = lax.psum_scatter(partial_sum, "src", scatter_dimension=0, tiled=True)
    acid_level = 1.0 - jnp.exp(-dose_scale * intensity)
    width_x = blur_x.shape[0]
    half_x = width_x // 2
    padded = jnp.pad(acid_level, ((0, 0), (half_x, half_x)))
    along_x = jnp.zeros_like(acid_level)
    for tap_index in range(width_x):
        along_x = (
            along_x + blur_x[tap_index] / width_x * padded[:, tap_index : tap_index + cols_tile]
        )
    width_y = blur_y.shape[0]
    half_y = width_y // 2
    extended = extended_2(along_x, (("src", 0),), half_y)
    along_y = jnp.zeros_like(along_x)
    for tap_index in range(width_y):
        along_y = along_y + blur_y[tap_index] / width_y * extended[tap_index : tap_index + own_rows]
    latent = blur_z[planes - 1] / planes * along_y
    for plane_lag in range(1 - planes, planes):
        if plane_lag != 0:
            arrived = passed_along(along_y, "src", plane_lag * per_plane)
            latent = latent + blur_z[plane_lag + planes - 1] / planes * arrived
    return (intensity, latent)


max_shift = 8
shifts = 2 * max_shift + 1
lanes = 512
devices_unrolled = 16


def exact_dot(left, right):
    def halves(value):
        high = value.astype(jnp.bfloat16)
        return high, (value - high.astype(jnp.float32)).astype(jnp.bfloat16)

    def product(a, b):
        return jnp.dot(a, b, preferred_element_type=jnp.float32)

    left_high, left_low = halves(left)
    right_high, right_low = halves(right)
    return (
        product(left_high, right_low) + product(left_low, right_high)
    ) + product(left_high, right_high)


def store_toeplitz(row, position, pieces, apart=128):
    base = pltpu.roll(jnp.broadcast_to(row, (16, 128)), 0, 1, stride=1, stride_axis=0)
    lane = lax.broadcasted_iota(jnp.int32, (16, 128), 1)
    zero = jnp.zeros((16, 128), jnp.float32)
    for j in range(8):
        first = 16 * j + position - 256
        turn, tile = first % 128, first // 128
        rolled = pltpu.roll(base, turn, 1) if turn else base
        wraps = turn > 65
        kept = jnp.where(lane >= turn, rolled, zero) if wraps else rolled
        wrapped = jnp.where(lane < turn, rolled, zero) if wraps else zero
        for block, start in ((j, tile), (j + 8, tile + 1)):
            for column in range(2):
                part = kept if column == start else wrapped if column == start + 1 else zero
                for ref, top, side, sign in pieces:
                    value = part if sign > 0 else -part
                    left = side + apart * column
                    ref[top + 16 * block : top + 16 * block + 16, left : left + 128] = (
                        value.astype(ref.dtype)
                    )


def store_taps(taps_ref, row, focus, flip, real_ref, imag_ref, tap_count):
    centre = (tap_count - 1) / 2.0
    amplitude = taps_ref[row : row + 1, :128] / math.sqrt(tap_count)
    shape = (24, 128)
    relative = (lax.broadcasted_iota(jnp.int32, shape, 1).astype(jnp.float32) - centre) * flip
    tilt = (lax.broadcasted_iota(jnp.int32, shape, 0) - max_shift).astype(jnp.float32)
    phase = (
        two_pi * tilt * relative / tap_count + defocus_scale * focus * (relative / centre) ** 2
    )
    real_ref[...] = amplitude * jnp.cos(phase)
    imag_ref[...] = amplitude * jnp.sin(phase)


def toeplitz_tiles(row, position, blocks):
    base = pltpu.roll(jnp.broadcast_to(row, (16, 128)), 0, 1, stride=1, stride_axis=0)
    apart = lax.broadcasted_iota(jnp.int32, (16, 128), 1) - lax.broadcasted_iota(
        jnp.int32, (16, 128), 0
    )
    tiles = {}
    for block in blocks:
        turn = 16 * block - position
        tile = pltpu.roll(base, turn % 128, 1) if turn % 128 else base
        if 127 - turn >= 128:
            tile = jnp.where(apart < 128 + turn, tile, 0.0)
        if -15 - turn < -80:
            tile = jnp.where(apart >= turn - 80, tile, 0.0)
        tiles[block] = tile
    return tiles


def build_columns(forward_real, forward_imag, shapes):
    def one_shift(shift):
        row = pl.ds(shift, 1)
        real = toeplitz_tiles(forward_real[row, :], 24, range(8))
        imag = toeplitz_tiles(forward_imag[row, :], 24, range(8))
        for j in range(8):
            re, im = real[j].astype(jnp.bfloat16), imag[j].astype(jnp.bfloat16)
            upper, lower = slice(16 * j, 16 * j + 16), slice(128 + 16 * j, 144 + 16 * j)
            shapes[shift, upper, :128] = re
            shapes[shift, upper, 128:] = -im
            shapes[shift, lower, :128] = im
            shapes[shift, lower, 128:] = re

    def four_shifts(step, carry):
        for place in range(4):
            one_shift(4 * step + place)
        return carry

    lax.fori_loop(0, shifts // 4, four_shifts, 0)
    one_shift(shifts - 1)


def build_fields(back_real, back_imag, mask_ref, slots, fields):
    mask_turned = mask_ref[...].astype(jnp.float32).T.astype(jnp.bfloat16)

    def one_shift(shift, slot):
        row = pl.ds(shift, 1)
        for side, source in ((0, back_real), (256, back_imag)):
            tiles = toeplitz_tiles(source[row, :], 23, range(-2, 10))
            for block, tile in tiles.items():
                value = tile.astype(jnp.bfloat16)
                if block >= 0:
                    slots[slot, 16 * block : 16 * block + 16, side : side + 128] = value
                if block < 8:
                    top = 16 * block + 128
                    slots[slot, top : top + 16, side + 128 : side + 256] = value
        fields[shift] = jnp.dot(
            mask_turned, slots[slot], preferred_element_type=jnp.float32
        ).astype(jnp.bfloat16)

    def four_shifts(step, carry):
        for slot in range(4):
            one_shift(4 * step + slot, slot)
        return carry

    lax.fori_loop(0, shifts // 4, four_shifts, 0)
    one_shift(shifts - 1, 0)


def lane_row(count, value):
    lane = lax.broadcasted_iota(jnp.int32, (1, lanes), 1)
    row = jnp.zeros((1, lanes), jnp.float32)
    for t in range(count):
        row = jnp.where(lane == t, value(t), row)
    return row


def plane_kernel(
    n, wide, mask_hbm, coords_hbm, weights_hbm, focus_hbm, taps_hbm, blur_x_hbm, blur_y_hbm,
    blur_z_hbm, intensity_ref, latent_ref, mask_ref, coords_ref, weights_ref, focus_ref, taps_ref,
    blur_x_ref, blur_y_ref, blur_z_ref, arg_sems, rows, t0, t1, t2, t3, slots, fields, shapes, image,
    acid, centre, mix, own, points, points_smem, along, columns, mixed, planes, send_sems, recv_sems,
    local_sem,
):
    me = lax.axis_index("src")
    group = lax.axis_index("groups")
    local = weights_ref.shape[0]
    tap_count, blur_count = taps_ref.shape[0], blur_x_ref.shape[0]
    barrier = pltpu.get_barrier_semaphore()

    def each(action):
        lax.fori_loop(1, n, lambda off, carry: (action(off), carry)[1], 0)

    def peer(off):
        return (group, lax.rem(me + off, n))

    def signal(off):
        pl.semaphore_signal(
            barrier, inc=1, device_id=peer(off), device_id_type=pl.DeviceIdType.MESH
        )

    def copy(phase, source, target, off, slot):
        return pltpu.make_async_remote_copy(
            src_ref=source(off),
            dst_ref=target.at[slot],
            send_sem=send_sems.at[phase, off],
            recv_sem=recv_sems.at[phase, off],
            device_id=peer(off),
            device_id_type=pl.DeviceIdType.MESH,
        )

    def start(phase, source, target):
        each(lambda off: copy(phase, source, target, off, me).start())

    def receive(phase, source, target):
        each(
            lambda off: copy(phase, source, target, off, lax.rem(me + n - off, n)).wait_recv()
        )

    def sent(phase, source, target):
        each(lambda off: copy(phase, source, target, off, me).wait_send())

    def blocks(ref, part):
        return lambda off: ref.at[part, lax.rem(me + off, n)]

    fetches = [
        pltpu.make_async_copy(source, target, arg_sems.at[place])
        for place, (source, target) in enumerate(
            (
                (coords_hbm, coords_ref),
                (weights_hbm, weights_ref),
                (focus_hbm, focus_ref),
                (taps_hbm, taps_ref),
                (blur_x_hbm, blur_x_ref),
                (blur_y_hbm, blur_y_ref),
                (blur_z_hbm, blur_z_ref),
                (mask_hbm, mask_ref),
            )
        )
    ]
    for fetch in fetches:
        fetch.start()
    each(signal)
    slots[...] = jnp.zeros_like(slots)
    for fetch in fetches:
        fetch.wait()
    lane = lax.broadcasted_iota(jnp.int32, (1, 128), 1)
    packed = jnp.zeros((1, 128), jnp.int32)
    for s in range(local):
        packed = jnp.where(lane == 3 * s, coords_ref[s, 0], packed)
        packed = jnp.where(lane == 3 * s + 1, coords_ref[s, 1], packed)
        packed = jnp.where(lane == 3 * s + 2, weights_ref[s], packed)
    own[...] = packed
    points[me] = packed
    rows[0:1, :] = lane_row(tap_count, lambda t: taps_ref[t])
    rows[1:2, :] = lane_row(tap_count, lambda t: taps_ref[tap_count - 1 - t])
    rows[2:3, :] = lane_row(blur_count, lambda t: blur_x_ref[t] / blur_count)
    rows[3:4, :] = lane_row(blur_count, lambda t: blur_y_ref[blur_count - 1 - t] / blur_count)
    focus = focus_ref[me].astype(jnp.float32)
    store_taps(rows, 0, focus, 1.0, t0, t1, tap_count)
    store_taps(rows, 1, focus, -1.0, t2, t3, tap_count)
    build_columns(t0, t1, shapes)
    pl.semaphore_wait(barrier, n - 1)
    point_source = lambda off: own
    start(0, point_source, points)
    build_fields(t2, t3, mask_ref, slots, fields)
    image[...] = jnp.zeros_like(image)
    tiles = toeplitz_tiles(rows[2:3, :128], 15, range(-1, 9))
    blank = jnp.zeros((96, 128), jnp.float32)
    blur_first = jnp.concatenate([tiles[j] for j in range(4)], axis=0)[:, :96]
    blur_last = jnp.concatenate([tiles[j] for j in range(2, 6)], axis=0)[:, :96]
    blur_middle = jnp.concatenate(
        [
            jnp.concatenate([tiles[j] for j in range(1, 9)], axis=0),
            jnp.concatenate([blank, tiles[-1], tiles[0]], axis=0)[:, :32],
        ],
        axis=1,
    )
    back_y = rows[3:4, :]
    store_toeplitz(rows[3:4, :128], 241, ((centre, 0, 0, 1),))
    tall = jnp.broadcast_to(back_y, (16, lanes))
    before = pltpu.roll(tall, lanes - 31, 1, stride=1, stride_axis=0)[:, :256]
    after = pltpu.roll(tall, 241, 1, stride=1, stride_axis=0)[:, :256]
    pad = jnp.zeros((112, 256), jnp.float32)
    size = n * wide
    distance = lax.broadcasted_iota(jnp.int32, (size, size), 0) - lax.broadcasted_iota(
        jnp.int32, (size, size), 1
    )
    mixing = jnp.zeros((size, size), jnp.float32)
    for lag in range(1 - n, n):
        mixing = jnp.where(distance == lag * wide, blur_z_ref[lag + n - 1] / n, mixing)
    mix[...] = mixing
    receive(0, point_source, points)
    to_smem = pltpu.make_async_copy(points, points_smem, local_sem)
    to_smem.start()
    to_smem.wait()

    def image_columns(left, low, high, first):
        count = high - low

        def some_devices(step, carry):
            power = jnp.zeros((count, 256), jnp.float32)
            for place in range(devices_unrolled * local):
                device, s = devices_unrolled * step + place // local, place % local
                point = [points_smem[device, 0, 3 * s + item] for item in range(3)]
                factor = point[2].astype(jnp.float32) / (4.0 * local * n)
                column, row = point[0] + max_shift, point[1] + max_shift
                field = jnp.dot(
                    jnp.concatenate(
                        [shapes[column, low:high], shapes[column, 128 + low : 128 + high]], axis=0
                    ),
                    jnp.concatenate(
                        [
                            fields[row, first : first + 128, :256],
                            fields[row, first : first + 128, 256:],
                        ],
                        axis=0,
                    ),
                    preferred_element_type=jnp.float32,
                )
                power = power + factor * (field[:count] ** 2 + field[count:] ** 2)
            image[left : left + count] += power
            return carry

        lax.fori_loop(0, n // devices_unrolled, some_devices, 0)
        acid[left : left + count] = 1.0 - jnp.exp(-dose_scale * image[left : left + count])

    def send_columns(part, values):
        along[part] = values.reshape(n, wide, 256)
        start(1 + part, blocks(along, part), columns.at[part])
        columns[part, me] = along[part, me]

    def mix_planes(part):
        receive(1 + part, blocks(along, part), columns.at[part])
        stack = columns[part].reshape(size, 256)
        zero = jnp.zeros((wide, 128), jnp.float32)
        along_y = (
            exact_dot(stack, centre[...])
            + exact_dot(
                jnp.concatenate([zero, stack[:-wide, 128:]], axis=0),
                jnp.concatenate([pad, before], axis=0),
            )
            + exact_dot(
                jnp.concatenate([stack[wide:, :128], zero], axis=0),
                jnp.concatenate([after, pad], axis=0),
            )
        )
        mixed[part] = exact_dot(mix[...], along_y).reshape(n, wide, 256)
        start(3 + part, blocks(mixed, part), planes.at[part])
        planes[part, me] = mixed[part, me]

    image_columns(0, 0, 96, 0)
    image_columns(160, 32, 128, 128)
    send_columns(
        0,
        jnp.concatenate(
            [exact_dot(blur_first, acid[:96]), exact_dot(blur_last, acid[160:])], axis=0
        ),
    )
    image_columns(96, 32, 96, 64)
    send_columns(1, exact_dot(blur_middle, acid[48:208]))
    intensity_ref[...] = image[...].T
    mix_planes(0)
    mix_planes(1)
    sent(0, point_source, points)
    receive(3, blocks(mixed, 0), planes.at[0])
    outer = planes[0].reshape(size, 256)
    latent_ref[:, :64] = outer[:64].T
    latent_ref[:, 192:] = outer[64:].T
    receive(4, blocks(mixed, 1), planes.at[1])
    latent_ref[:, 64:192] = planes[1].reshape(size, 256).T
    for part in range(2):
        sent(1 + part, blocks(along, part), columns.at[part])
        sent(3 + part, blocks(mixed, part), planes.at[part])


def store_kernel(intensity_ref, latent_ref, intensity_hbm, latent_hbm, sems):
    stores = [
        pltpu.make_async_copy(intensity_ref, intensity_hbm, sems.at[0]),
        pltpu.make_async_copy(latent_ref, latent_hbm, sems.at[1]),
    ]
    for store in stores:
        store.start()
    for store in stores:
        store.wait()


def plane_per_device(
    layout_mask, source_coords, source_weights, focus_steps, pupil_taps, blur_x, blur_y, blur_z
):
    n = lax.axis_size("src")
    wide = layout_mask.shape[1] // n // 2
    square = jax.ShapeDtypeStruct((256, 256), jnp.float32)
    full = pltpu.VMEM((256, 256), jnp.float32)
    parts = pltpu.VMEM((2, n, wide, 256), jnp.float32)
    vmem = pl.BlockSpec(memory_space=pltpu.VMEM)
    hbm = pl.BlockSpec(memory_space=pltpu.HBM)
    arguments = (
        source_coords, source_weights, focus_steps, pupil_taps, blur_x, blur_y, blur_z
    )
    made = pl.pallas_call(
        lambda *refs: plane_kernel(n, wide, *refs),
        out_shape=(square, square),
        in_specs=[hbm] * 8,
        out_specs=(vmem, vmem),
        scratch_shapes=[pltpu.VMEM((256, 256), jnp.int32)]
        + [pltpu.SMEM(value.shape, value.dtype) for value in arguments]
        + [pltpu.SemaphoreType.DMA((8,)), pltpu.VMEM((8, lanes), jnp.float32)]
        + [pltpu.VMEM((24, 128), jnp.float32)] * 4
        + [
            pltpu.VMEM((4, 256, 512), jnp.bfloat16),
            pltpu.VMEM((shifts, 256, 512), jnp.bfloat16),
            pltpu.VMEM((shifts, 256, 256), jnp.bfloat16),
            full,
            full,
            full,
            pltpu.VMEM((n * wide, n * wide), jnp.float32),
            pltpu.VMEM((1, 128), jnp.int32),
            pltpu.VMEM((n, 1, 128), jnp.int32),
            pltpu.SMEM((n, 1, 128), jnp.int32),
            parts,
            parts,
            parts,
            parts,
            pltpu.SemaphoreType.DMA((5, n)),
            pltpu.SemaphoreType.DMA((5, n)),
            pltpu.SemaphoreType.DMA,
        ],
        compiler_params=pltpu.CompilerParams(
            vmem_limit_bytes=32 * 2**20, collective_id=0, has_side_effects=True
        ),
    )(*[pltpu.with_memory_space_constraint(value, pltpu.HBM) for value in (layout_mask, *arguments)])
    return pl.pallas_call(
        store_kernel,
        out_shape=(square, square),
        in_specs=[vmem] * 2,
        out_specs=(hbm, hbm),
        scratch_shapes=[pltpu.SemaphoreType.DMA((2,))],
    )(*[pltpu.with_memory_space_constraint(value, pltpu.VMEM) for value in made])


def solution(mesh):
    in_specs = (P("groups", None), P("src", None), P("src"), P(), P(), P(), P(), P())
    out_specs = (P(("groups", "src"), None), P(("groups", "src"), None))
    body = plane_per_device if mesh.shape["src"] == 16 else on_device
    return jax.shard_map(
        body, mesh=mesh, in_specs=in_specs, out_specs=out_specs, check_vma=False
    )
```

```python
import math

import jax
import jax.numpy as jnp
from jax import lax
from jax.experimental import pallas as pl
from jax.experimental.pallas import tpu as pltpu
from jax.sharding import PartitionSpec as P

two_pi = 2.0 * math.pi
defocus_scale = 0.8
dose_scale = 2.0


def extended_2(block, sides, width):
    for axis, dim in sides:
        count = lax.axis_size(axis)
        forward = [(i, i + 1) for i in range(count - 1)]
        backward = [(target, source) for source, target in forward]
        low = lax.ppermute(
            lax.slice_in_dim(block, block.shape[dim] - width, None, axis=dim), axis, forward
        )
        high = lax.ppermute(lax.slice_in_dim(block, 0, width, axis=dim), axis, backward)
        block = jnp.concatenate([low, block, high], axis=dim)
    return block


def passed_along(block, axis, distance):
    devices = range(lax.axis_size(axis))
    route = [(i - distance, i) for i in devices if i - distance in devices]
    return lax.ppermute(block, axis, route)


def tap_matrix(out_pos, extent, tilt_index, focus_step, pupil_taps):
    tap_count = pupil_taps.shape[0]
    centre = (tap_count - 1) / 2.0
    column_pos = jnp.arange(extent, dtype=jnp.int32)
    offset = column_pos[None, :] - out_pos[:, None] + tap_count // 2
    inside = (offset >= 0) & (offset < tap_count)
    clipped = jnp.clip(offset, 0, tap_count - 1)
    amplitude = jnp.take(pupil_taps, clipped) / math.sqrt(tap_count)
    relative = clipped.astype(jnp.float32) - centre
    phase_angle = (
        two_pi * tilt_index.astype(jnp.float32) * relative / tap_count
        + defocus_scale * focus_step.astype(jnp.float32) * (relative / centre) ** 2
    )
    real_part = jnp.where(inside, amplitude * jnp.cos(phase_angle), jnp.zeros_like(amplitude))
    imag_part = jnp.where(inside, amplitude * jnp.sin(phase_angle), jnp.zeros_like(amplitude))
    return (real_part.astype(jnp.bfloat16), imag_part.astype(jnp.bfloat16))


def field_power(mask_bf, row_pos, tilt_x, tilt_y, focus_step, pupil_taps):
    rows_tile, cols_tile = mask_bf.shape
    row_count = row_pos.shape[0]
    col_pos = jnp.arange(cols_tile, dtype=jnp.int32)
    rows_real, rows_imag = tap_matrix(row_pos, rows_tile, tilt_y, focus_step, pupil_taps)
    cols_real, cols_imag = tap_matrix(col_pos, cols_tile, tilt_x, focus_step, pupil_taps)
    stacked = jnp.concatenate([rows_real, rows_imag], axis=0)
    first_pass = jnp.dot(stacked, mask_bf, preferred_element_type=jnp.float32).astype(jnp.bfloat16)
    joined = jnp.concatenate([first_pass[:row_count], first_pass[row_count:]], axis=1)
    upper_half = jnp.concatenate([cols_real.T, cols_imag.T], axis=1)
    lower_half = jnp.concatenate([-cols_imag.T, cols_real.T], axis=1)
    pupil_cols = jnp.concatenate([upper_half, lower_half], axis=0)
    field_parts = jnp.dot(joined, pupil_cols, preferred_element_type=jnp.float32)
    return field_parts[:, :cols_tile] ** 2 + field_parts[:, cols_tile:] ** 2


def on_device(
    layout_mask, source_coords, source_weights, focus_steps, pupil_taps, blur_x, blur_y, blur_z
):
    rows_tile, cols_tile = layout_mask.shape
    planes = focus_steps.shape[0]
    devices = lax.axis_size("src")
    src_local = source_coords.shape[0]
    mask_bf = layout_mask.astype(jnp.bfloat16)
    own_rows = planes * rows_tile // devices
    per_plane = devices // planes
    factors = source_weights.astype(jnp.float32) / (4.0 * src_local * devices)
    row_pos = jnp.arange(rows_tile, dtype=jnp.int32)

    def plane_term(focus_step):
        running = jnp.zeros((rows_tile, cols_tile), jnp.float32)
        for source in range(src_local):
            power = field_power(
                mask_bf,
                row_pos,
                source_coords[source, 0],
                source_coords[source, 1],
                focus_step,
                pupil_taps,
            )
            running = running + factors[source] * power
        return running

    partial_sum = lax.map(plane_term, focus_steps).reshape(planes * rows_tile, cols_tile)
    intensity = lax.psum_scatter(partial_sum, "src", scatter_dimension=0, tiled=True)
    acid_level = 1.0 - jnp.exp(-dose_scale * intensity)
    width_x = blur_x.shape[0]
    half_x = width_x // 2
    padded = jnp.pad(acid_level, ((0, 0), (half_x, half_x)))
    along_x = jnp.zeros_like(acid_level)
    for tap_index in range(width_x):
        along_x = (
            along_x + blur_x[tap_index] / width_x * padded[:, tap_index : tap_index + cols_tile]
        )
    width_y = blur_y.shape[0]
    half_y = width_y // 2
    extended = extended_2(along_x, (("src", 0),), half_y)
    along_y = jnp.zeros_like(along_x)
    for tap_index in range(width_y):
        along_y = along_y + blur_y[tap_index] / width_y * extended[tap_index : tap_index + own_rows]
    latent = blur_z[planes - 1] / planes * along_y
    for plane_lag in range(1 - planes, planes):
        if plane_lag != 0:
            arrived = passed_along(along_y, "src", plane_lag * per_plane)
            latent = latent + blur_z[plane_lag + planes - 1] / planes * arrived
    return (intensity, latent)


max_shift = 8
shifts = 2 * max_shift + 1
lanes = 512
devices_unrolled = 16


def exact_dot(left, right):
    def halves(value):
        high = value.astype(jnp.bfloat16)
        return high, (value - high.astype(jnp.float32)).astype(jnp.bfloat16)

    def product(a, b):
        return jnp.dot(a, b, preferred_element_type=jnp.float32)

    left_high, left_low = halves(left)
    right_high, right_low = halves(right)
    return (
        product(left_high, right_low) + product(left_low, right_high)
    ) + product(left_high, right_high)


def store_toeplitz(row, position, pieces, apart=128):
    base = pltpu.roll(jnp.broadcast_to(row, (16, 128)), 0, 1, stride=1, stride_axis=0)
    lane = lax.broadcasted_iota(jnp.int32, (16, 128), 1)
    zero = jnp.zeros((16, 128), jnp.float32)
    for j in range(8):
        first = 16 * j + position - 256
        turn, tile = first % 128, first // 128
        rolled = pltpu.roll(base, turn, 1) if turn else base
        wraps = turn > 65
        kept = jnp.where(lane >= turn, rolled, zero) if wraps else rolled
        wrapped = jnp.where(lane < turn, rolled, zero) if wraps else zero
        for block, start in ((j, tile), (j + 8, tile + 1)):
            for column in range(2):
                part = kept if column == start else wrapped if column == start + 1 else zero
                for ref, top, side, sign in pieces:
                    value = part if sign > 0 else -part
                    left = side + apart * column
                    ref[top + 16 * block : top + 16 * block + 16, left : left + 128] = (
                        value.astype(ref.dtype)
                    )


def store_taps(taps_ref, row, focus, flip, real_ref, imag_ref, tap_count):
    centre = (tap_count - 1) / 2.0
    amplitude = taps_ref[row : row + 1, :128] / math.sqrt(tap_count)
    shape = (24, 128)
    relative = (lax.broadcasted_iota(jnp.int32, shape, 1).astype(jnp.float32) - centre) * flip
    tilt = (lax.broadcasted_iota(jnp.int32, shape, 0) - max_shift).astype(jnp.float32)
    phase = (
        two_pi * tilt * relative / tap_count + defocus_scale * focus * (relative / centre) ** 2
    )
    real_ref[...] = amplitude * jnp.cos(phase)
    imag_ref[...] = amplitude * jnp.sin(phase)


def toeplitz_tiles(row, position, blocks, dtype=jnp.float32):
    base = pltpu.roll(jnp.broadcast_to(row, (16, 128)), 0, 1, stride=1, stride_axis=0)
    apart = lax.broadcasted_iota(jnp.int32, (16, 128), 1) - lax.broadcasted_iota(
        jnp.int32, (16, 128), 0
    )
    base = base.astype(dtype)
    tiles = {}
    for block in blocks:
        turn = 16 * block - position
        tile = pltpu.roll(base, turn % 128, 1) if turn % 128 else base
        if 127 - turn >= 128:
            tile = jnp.where(apart < 128 + turn, tile, jnp.zeros_like(tile))
        if -15 - turn < -80:
            tile = jnp.where(apart >= turn - 80, tile, jnp.zeros_like(tile))
        tiles[block] = tile
    return tiles


def build_tables(forward_real, forward_imag, back_real, back_imag, mask_ref, slots, shapes, fields):
    mask_turned = mask_ref[...].astype(jnp.float32).T.astype(jnp.bfloat16)

    def one_shift(shift, slot):
        row = pl.ds(shift, 1)
        real = toeplitz_tiles(forward_real[row, :], 24, range(8), jnp.bfloat16)
        imag = toeplitz_tiles(forward_imag[row, :], 24, range(8), jnp.bfloat16)
        for j in range(8):
            upper, lower = slice(16 * j, 16 * j + 16), slice(128 + 16 * j, 144 + 16 * j)
            shapes[shift, upper, :128] = real[j]
            shapes[shift, upper, 128:] = -imag[j]
            shapes[shift, lower, :128] = imag[j]
            shapes[shift, lower, 128:] = real[j]
        for side, source in ((0, back_real), (256, back_imag)):
            tiles = toeplitz_tiles(source[row, :], 23, range(-2, 10), jnp.bfloat16)
            for block, tile in tiles.items():
                if block >= 0:
                    slots[slot, 16 * block : 16 * block + 16, side : side + 128] = tile
                if block < 8:
                    top = 16 * block + 128
                    slots[slot, top : top + 16, side + 128 : side + 256] = tile
        for side in (0, 256):
            fields[shift, :, side : side + 256] = jnp.dot(
                mask_turned, slots[slot, :, side : side + 256], preferred_element_type=jnp.float32
            ).astype(jnp.bfloat16)

    for shift in range(shifts):
        one_shift(shift, shift % 4)


def lane_row(count, value):
    lane = lax.broadcasted_iota(jnp.int32, (1, lanes), 1)
    row = jnp.zeros((1, lanes), jnp.float32)
    for t in range(count):
        row = jnp.where(lane == t, value(t), row)
    return row


def plane_kernel(
    n, wide, mask_hbm, coords_hbm, weights_hbm, focus_hbm, taps_hbm, blur_x_hbm, blur_y_hbm,
    blur_z_hbm, intensity_ref, latent_ref, mask_ref, coords_ref, weights_ref, focus_ref, taps_ref,
    blur_x_ref, blur_y_ref, blur_z_ref, arg_sems, rows, t0, t1, t2, t3, slots, fields, shapes, image,
    acid, centre, mix, own, points, points_smem, along, columns, mixed, planes, send_sems, recv_sems,
    local_sem,
):
    me = lax.axis_index("src")
    group = lax.axis_index("groups")
    local = weights_ref.shape[0]
    tap_count, blur_count = taps_ref.shape[0], blur_x_ref.shape[0]
    barrier = pltpu.get_barrier_semaphore()

    def each(action):
        lax.fori_loop(1, n, lambda off, carry: (action(off), carry)[1], 0)

    def peer(off):
        return (group, lax.rem(me + off, n))

    def signal(off):
        pl.semaphore_signal(
            barrier, inc=1, device_id=peer(off), device_id_type=pl.DeviceIdType.MESH
        )

    def copy(phase, source, target, off, slot):
        return pltpu.make_async_remote_copy(
            src_ref=source(off),
            dst_ref=target.at[slot],
            send_sem=send_sems.at[phase],
            recv_sem=recv_sems.at[phase],
            device_id=peer(off),
            device_id_type=pl.DeviceIdType.MESH,
        )

    def start(phase, source, target):
        each(lambda off: copy(phase, source, target, off, me).start())

    def whole(phase, target):
        others = target.at[pl.ds(0, n - 1)]
        return pltpu.make_async_remote_copy(
            src_ref=others,
            dst_ref=others,
            send_sem=send_sems.at[phase],
            recv_sem=recv_sems.at[phase],
            device_id=peer(1),
            device_id_type=pl.DeviceIdType.MESH,
        )

    def receive(phase, target):
        whole(phase, target).wait_recv()

    def sent(phase, target):
        whole(phase, target).wait_send()

    def blocks(ref, part):
        return lambda off: ref.at[part, lax.rem(me + off, n)]

    fetches = [
        pltpu.make_async_copy(source, target, arg_sems.at[place])
        for place, (source, target) in enumerate(
            (
                (coords_hbm, coords_ref),
                (weights_hbm, weights_ref),
                (focus_hbm, focus_ref),
                (taps_hbm, taps_ref),
                (blur_x_hbm, blur_x_ref),
                (blur_y_hbm, blur_y_ref),
                (blur_z_hbm, blur_z_ref),
                (mask_hbm, mask_ref),
            )
        )
    ]
    for fetch in fetches:
        fetch.start()
    each(signal)
    slots[...] = jnp.zeros_like(slots)
    for fetch in fetches:
        fetch.wait()
    lane = lax.broadcasted_iota(jnp.int32, (1, 128), 1)
    packed = jnp.zeros((1, 128), jnp.int32)
    for s in range(local):
        packed = jnp.where(lane == 3 * s, coords_ref[s, 0], packed)
        packed = jnp.where(lane == 3 * s + 1, coords_ref[s, 1], packed)
        packed = jnp.where(lane == 3 * s + 2, weights_ref[s], packed)
    own[...] = packed
    points[me] = packed
    rows[0:1, :] = lane_row(tap_count, lambda t: taps_ref[t])
    rows[1:2, :] = lane_row(tap_count, lambda t: taps_ref[tap_count - 1 - t])
    rows[2:3, :] = lane_row(blur_count, lambda t: blur_x_ref[t] / blur_count)
    rows[3:4, :] = lane_row(blur_count, lambda t: blur_y_ref[blur_count - 1 - t] / blur_count)
    focus = focus_ref[me].astype(jnp.float32)
    store_taps(rows, 0, focus, 1.0, t0, t1, tap_count)
    store_taps(rows, 1, focus, -1.0, t2, t3, tap_count)
    pl.semaphore_wait(barrier, n - 1)
    point_source = lambda off: own
    each(lambda off: copy(0, point_source, points, n - off, me).start())
    build_tables(t0, t1, t2, t3, mask_ref, slots, shapes, fields)
    image[...] = jnp.zeros_like(image)
    tiles = toeplitz_tiles(rows[2:3, :128], 15, range(-1, 9))
    blank = jnp.zeros((96, 128), jnp.float32)
    blur_first = jnp.concatenate([tiles[j] for j in range(4)], axis=0)[:, :96]
    blur_last = jnp.concatenate([tiles[j] for j in range(2, 6)], axis=0)[:, :96]
    blur_middle = jnp.concatenate(
        [
            jnp.concatenate([tiles[j] for j in range(1, 9)], axis=0),
            jnp.concatenate([blank, tiles[-1], tiles[0]], axis=0)[:, :32],
        ],
        axis=1,
    )
    back_y = rows[3:4, :]
    store_toeplitz(rows[3:4, :128], 241, ((centre, 0, 0, 1),))
    tall = jnp.broadcast_to(back_y, (16, lanes))
    before = pltpu.roll(tall, lanes - 31, 1, stride=1, stride_axis=0)[:, :256]
    after = pltpu.roll(tall, 241, 1, stride=1, stride_axis=0)[:, :256]
    pad = jnp.zeros((112, 256), jnp.float32)
    size = n * wide
    distance = lax.broadcasted_iota(jnp.int32, (size, size), 0) - lax.broadcasted_iota(
        jnp.int32, (size, size), 1
    )
    mixing = jnp.zeros((size, size), jnp.float32)
    for lag in range(1 - n, n):
        mixing = jnp.where(distance == lag * wide, blur_z_ref[lag + n - 1] / n, mixing)
    mix[...] = mixing
    receive(0, points)
    to_smem = pltpu.make_async_copy(points, points_smem, local_sem)
    to_smem.start()
    to_smem.wait()

    def image_columns(left, low, high, first):
        count = high - low

        def some_devices(step, carry):
            power = jnp.zeros((count, 256), jnp.float32)
            for place in range(devices_unrolled * local):
                device, s = devices_unrolled * step + place // local, place % local
                point = [points_smem[device, 0, 3 * s + item] for item in range(3)]
                factor = point[2].astype(jnp.float32) / (4.0 * local * n)
                column, row = point[0] + max_shift, point[1] + max_shift
                field = jnp.dot(
                    jnp.concatenate(
                        [shapes[column, low:high], shapes[column, 128 + low : 128 + high]], axis=0
                    ),
                    jnp.concatenate(
                        [
                            fields[row, first : first + 128, :256],
                            fields[row, first : first + 128, 256:],
                        ],
                        axis=0,
                    ),
                    preferred_element_type=jnp.float32,
                )
                power = power + factor * (field[:count] ** 2 + field[count:] ** 2)
            image[left : left + count] += power
            return carry

        lax.fori_loop(0, n // devices_unrolled, some_devices, 0)
        acid[left : left + count] = 1.0 - jnp.exp(-dose_scale * image[left : left + count])

    def send_columns(part, values):
        along[part] = values.reshape(n, wide, 256)
        start(1 + part, blocks(along, part), columns.at[part])
        columns[part, me] = along[part, me]

    def mix_planes(part):
        receive(1 + part, columns.at[part])
        stack = columns[part].reshape(size, 256)
        zero = jnp.zeros((wide, 128), jnp.float32)
        along_y = (
            exact_dot(stack, centre[...])
            + exact_dot(
                jnp.concatenate([zero, stack[:-wide, 128:]], axis=0),
                jnp.concatenate([pad, before], axis=0),
            )
            + exact_dot(
                jnp.concatenate([stack[wide:, :128], zero], axis=0),
                jnp.concatenate([after, pad], axis=0),
            )
        )
        mixed[part] = exact_dot(mix[...], along_y).reshape(n, wide, 256)
        start(3 + part, blocks(mixed, part), planes.at[part])
        planes[part, me] = mixed[part, me]

    image_columns(0, 0, 96, 0)
    image_columns(160, 32, 128, 128)
    send_columns(
        0,
        jnp.concatenate(
            [exact_dot(blur_first, acid[:96]), exact_dot(blur_last, acid[160:])], axis=0
        ),
    )
    image_columns(96, 32, 96, 64)
    send_columns(1, exact_dot(blur_middle, acid[48:208]))
    intensity_ref[...] = image[...].T
    mix_planes(0)
    mix_planes(1)
    sent(0, points)
    sent(1, columns.at[0])
    sent(2, columns.at[1])
    sent(3, planes.at[0])
    receive(3, planes.at[0])
    outer = planes[0].reshape(size, 256)
    latent_ref[:, :64] = outer[:64].T
    latent_ref[:, 192:] = outer[64:].T
    sent(4, planes.at[1])
    receive(4, planes.at[1])
    latent_ref[:, 64:192] = planes[1].reshape(size, 256).T


def store_kernel(intensity_ref, latent_ref, intensity_hbm, latent_hbm, sems):
    stores = [
        pltpu.make_async_copy(intensity_ref, intensity_hbm, sems.at[0]),
        pltpu.make_async_copy(latent_ref, latent_hbm, sems.at[1]),
    ]
    for store in stores:
        store.start()
    for store in stores:
        store.wait()


def plane_per_device(
    layout_mask, source_coords, source_weights, focus_steps, pupil_taps, blur_x, blur_y, blur_z
):
    n = lax.axis_size("src")
    wide = layout_mask.shape[1] // n // 2
    square = jax.ShapeDtypeStruct((256, 256), jnp.float32)
    full = pltpu.VMEM((256, 256), jnp.float32)
    parts = pltpu.VMEM((2, n, wide, 256), jnp.float32)
    vmem = pl.BlockSpec(memory_space=pltpu.VMEM)
    hbm = pl.BlockSpec(memory_space=pltpu.HBM)
    arguments = (
        source_coords, source_weights, focus_steps, pupil_taps, blur_x, blur_y, blur_z
    )
    made = pl.pallas_call(
        lambda *refs: plane_kernel(n, wide, *refs),
        out_shape=(square, square),
        in_specs=[hbm] * 8,
        out_specs=(vmem, vmem),
        scratch_shapes=[pltpu.VMEM((256, 256), jnp.int32)]
        + [pltpu.SMEM(value.shape, value.dtype) for value in arguments]
        + [pltpu.SemaphoreType.DMA((8,)), pltpu.VMEM((8, lanes), jnp.float32)]
        + [pltpu.VMEM((24, 128), jnp.float32)] * 4
        + [
            pltpu.VMEM((4, 256, 512), jnp.bfloat16),
            pltpu.VMEM((shifts, 256, 512), jnp.bfloat16),
            pltpu.VMEM((shifts, 256, 256), jnp.bfloat16),
            full,
            full,
            full,
            pltpu.VMEM((n * wide, n * wide), jnp.float32),
            pltpu.VMEM((1, 128), jnp.int32),
            pltpu.VMEM((n, 1, 128), jnp.int32),
            pltpu.SMEM((n, 1, 128), jnp.int32),
            parts,
            parts,
            parts,
            parts,
            pltpu.SemaphoreType.DMA((5,)),
            pltpu.SemaphoreType.DMA((5,)),
            pltpu.SemaphoreType.DMA,
        ],
        compiler_params=pltpu.CompilerParams(
            vmem_limit_bytes=32 * 2**20, collective_id=0, has_side_effects=True
        ),
    )(*[pltpu.with_memory_space_constraint(value, pltpu.HBM) for value in (layout_mask, *arguments)])
    return pl.pallas_call(
        store_kernel,
        out_shape=(square, square),
        in_specs=[vmem] * 2,
        out_specs=(hbm, hbm),
        scratch_shapes=[pltpu.SemaphoreType.DMA((2,))],
    )(*[pltpu.with_memory_space_constraint(value, pltpu.VMEM) for value in made])


def solution(mesh):
    in_specs = (P("groups", None), P("src", None), P("src"), P(), P(), P(), P(), P())
    out_specs = (P(("groups", "src"), None), P(("groups", "src"), None))
    body = plane_per_device if mesh.shape["src"] == 16 else on_device
    return jax.shard_map(
        body, mesh=mesh, in_specs=in_specs, out_specs=out_specs, check_vma=False
    )
```

```python
import math

import jax
import jax.numpy as jnp
from jax import lax
from jax.experimental import pallas as pl
from jax.experimental.pallas import tpu as pltpu
from jax.sharding import PartitionSpec as P

two_pi = 2.0 * math.pi
defocus_scale = 0.8
dose_scale = 2.0


def extended_2(block, sides, width):
    for axis, dim in sides:
        count = lax.axis_size(axis)
        forward = [(i, i + 1) for i in range(count - 1)]
        backward = [(target, source) for source, target in forward]
        low = lax.ppermute(
            lax.slice_in_dim(block, block.shape[dim] - width, None, axis=dim), axis, forward
        )
        high = lax.ppermute(lax.slice_in_dim(block, 0, width, axis=dim), axis, backward)
        block = jnp.concatenate([low, block, high], axis=dim)
    return block


def passed_along(block, axis, distance):
    devices = range(lax.axis_size(axis))
    route = [(i - distance, i) for i in devices if i - distance in devices]
    return lax.ppermute(block, axis, route)


def tap_matrix(out_pos, extent, tilt_index, focus_step, pupil_taps):
    tap_count = pupil_taps.shape[0]
    centre = (tap_count - 1) / 2.0
    column_pos = jnp.arange(extent, dtype=jnp.int32)
    offset = column_pos[None, :] - out_pos[:, None] + tap_count // 2
    inside = (offset >= 0) & (offset < tap_count)
    clipped = jnp.clip(offset, 0, tap_count - 1)
    amplitude = jnp.take(pupil_taps, clipped) / math.sqrt(tap_count)
    relative = clipped.astype(jnp.float32) - centre
    phase_angle = (
        two_pi * tilt_index.astype(jnp.float32) * relative / tap_count
        + defocus_scale * focus_step.astype(jnp.float32) * (relative / centre) ** 2
    )
    real_part = jnp.where(inside, amplitude * jnp.cos(phase_angle), jnp.zeros_like(amplitude))
    imag_part = jnp.where(inside, amplitude * jnp.sin(phase_angle), jnp.zeros_like(amplitude))
    return (real_part.astype(jnp.bfloat16), imag_part.astype(jnp.bfloat16))


def field_power(mask_bf, row_pos, tilt_x, tilt_y, focus_step, pupil_taps):
    rows_tile, cols_tile = mask_bf.shape
    row_count = row_pos.shape[0]
    col_pos = jnp.arange(cols_tile, dtype=jnp.int32)
    rows_real, rows_imag = tap_matrix(row_pos, rows_tile, tilt_y, focus_step, pupil_taps)
    cols_real, cols_imag = tap_matrix(col_pos, cols_tile, tilt_x, focus_step, pupil_taps)
    stacked = jnp.concatenate([rows_real, rows_imag], axis=0)
    first_pass = jnp.dot(stacked, mask_bf, preferred_element_type=jnp.float32).astype(jnp.bfloat16)
    joined = jnp.concatenate([first_pass[:row_count], first_pass[row_count:]], axis=1)
    upper_half = jnp.concatenate([cols_real.T, cols_imag.T], axis=1)
    lower_half = jnp.concatenate([-cols_imag.T, cols_real.T], axis=1)
    pupil_cols = jnp.concatenate([upper_half, lower_half], axis=0)
    field_parts = jnp.dot(joined, pupil_cols, preferred_element_type=jnp.float32)
    return field_parts[:, :cols_tile] ** 2 + field_parts[:, cols_tile:] ** 2


def on_device(
    layout_mask, source_coords, source_weights, focus_steps, pupil_taps, blur_x, blur_y, blur_z
):
    rows_tile, cols_tile = layout_mask.shape
    planes = focus_steps.shape[0]
    devices = lax.axis_size("src")
    src_local = source_coords.shape[0]
    mask_bf = layout_mask.astype(jnp.bfloat16)
    own_rows = planes * rows_tile // devices
    per_plane = devices // planes
    factors = source_weights.astype(jnp.float32) / (4.0 * src_local * devices)
    row_pos = jnp.arange(rows_tile, dtype=jnp.int32)

    def plane_term(focus_step):
        running = jnp.zeros((rows_tile, cols_tile), jnp.float32)
        for source in range(src_local):
            power = field_power(
                mask_bf,
                row_pos,
                source_coords[source, 0],
                source_coords[source, 1],
                focus_step,
                pupil_taps,
            )
            running = running + factors[source] * power
        return running

    partial_sum = lax.map(plane_term, focus_steps).reshape(planes * rows_tile, cols_tile)
    intensity = lax.psum_scatter(partial_sum, "src", scatter_dimension=0, tiled=True)
    acid_level = 1.0 - jnp.exp(-dose_scale * intensity)
    width_x = blur_x.shape[0]
    half_x = width_x // 2
    padded = jnp.pad(acid_level, ((0, 0), (half_x, half_x)))
    along_x = jnp.zeros_like(acid_level)
    for tap_index in range(width_x):
        along_x = (
            along_x + blur_x[tap_index] / width_x * padded[:, tap_index : tap_index + cols_tile]
        )
    width_y = blur_y.shape[0]
    half_y = width_y // 2
    extended = extended_2(along_x, (("src", 0),), half_y)
    along_y = jnp.zeros_like(along_x)
    for tap_index in range(width_y):
        along_y = along_y + blur_y[tap_index] / width_y * extended[tap_index : tap_index + own_rows]
    latent = blur_z[planes - 1] / planes * along_y
    for plane_lag in range(1 - planes, planes):
        if plane_lag != 0:
            arrived = passed_along(along_y, "src", plane_lag * per_plane)
            latent = latent + blur_z[plane_lag + planes - 1] / planes * arrived
    return (intensity, latent)


max_shift = 8
shifts = 2 * max_shift + 1
lanes = 512
devices_unrolled = 16


def exact_dot(left, right):
    def halves(value):
        high = value.astype(jnp.bfloat16)
        return high, (value - high.astype(jnp.float32)).astype(jnp.bfloat16)

    def product(a, b):
        return jnp.dot(a, b, preferred_element_type=jnp.float32)

    left_high, left_low = halves(left)
    right_high, right_low = halves(right)
    return (
        product(left_high, right_low) + product(left_low, right_high)
    ) + product(left_high, right_high)


def store_toeplitz(row, position, pieces, apart=128):
    base = pltpu.roll(jnp.broadcast_to(row, (16, 128)), 0, 1, stride=1, stride_axis=0)
    lane = lax.broadcasted_iota(jnp.int32, (16, 128), 1)
    zero = jnp.zeros((16, 128), jnp.float32)
    for j in range(8):
        first = 16 * j + position - 256
        turn, tile = first % 128, first // 128
        rolled = pltpu.roll(base, turn, 1) if turn else base
        wraps = turn > 65
        kept = jnp.where(lane >= turn, rolled, zero) if wraps else rolled
        wrapped = jnp.where(lane < turn, rolled, zero) if wraps else zero
        for block, start in ((j, tile), (j + 8, tile + 1)):
            for column in range(2):
                part = kept if column == start else wrapped if column == start + 1 else zero
                for ref, top, side, sign in pieces:
                    value = part if sign > 0 else -part
                    left = side + apart * column
                    ref[top + 16 * block : top + 16 * block + 16, left : left + 128] = (
                        value.astype(ref.dtype)
                    )


def store_taps(taps_ref, row, focus, flip, real_ref, imag_ref, tap_count):
    centre = (tap_count - 1) / 2.0
    amplitude = taps_ref[row : row + 1, :128] / math.sqrt(tap_count)
    shape = (24, 128)
    relative = (lax.broadcasted_iota(jnp.int32, shape, 1).astype(jnp.float32) - centre) * flip
    tilt = (lax.broadcasted_iota(jnp.int32, shape, 0) - max_shift).astype(jnp.float32)
    phase = (
        two_pi * tilt * relative / tap_count + defocus_scale * focus * (relative / centre) ** 2
    )
    real_ref[...] = amplitude * jnp.cos(phase)
    imag_ref[...] = amplitude * jnp.sin(phase)


def toeplitz_tiles(row, position, blocks, dtype=jnp.float32):
    base = pltpu.roll(jnp.broadcast_to(row, (16, 128)), 0, 1, stride=1, stride_axis=0)
    apart = lax.broadcasted_iota(jnp.int32, (16, 128), 1) - lax.broadcasted_iota(
        jnp.int32, (16, 128), 0
    )
    base = base.astype(dtype)
    tiles = {}
    for block in blocks:
        turn = 16 * block - position
        tile = pltpu.roll(base, turn % 128, 1) if turn % 128 else base
        if 127 - turn >= 128:
            tile = jnp.where(apart < 128 + turn, tile, jnp.zeros_like(tile))
        if -15 - turn < -80:
            tile = jnp.where(apart >= turn - 80, tile, jnp.zeros_like(tile))
        tiles[block] = tile
    return tiles


def build_tables(forward_real, forward_imag, back_real, back_imag, mask_ref, slots, shapes, fields):
    mask_turned = mask_ref[...].astype(jnp.float32).T.astype(jnp.bfloat16)

    def one_shift(shift, slot):
        row = pl.ds(shift, 1)
        real = toeplitz_tiles(forward_real[row, :], 24, range(8), jnp.bfloat16)
        imag = toeplitz_tiles(forward_imag[row, :], 24, range(8), jnp.bfloat16)
        for j in range(8):
            upper, lower = slice(16 * j, 16 * j + 16), slice(128 + 16 * j, 144 + 16 * j)
            shapes[shift, upper, :128] = real[j]
            shapes[shift, upper, 128:] = -imag[j]
            shapes[shift, lower, :128] = imag[j]
            shapes[shift, lower, 128:] = real[j]
        for side, source in ((0, back_real), (256, back_imag)):
            tiles = toeplitz_tiles(source[row, :], 23, range(-2, 10), jnp.bfloat16)
            for block, tile in tiles.items():
                if block >= 0:
                    slots[slot, 16 * block : 16 * block + 16, side : side + 128] = tile
                if block < 8:
                    top = 16 * block + 128
                    slots[slot, top : top + 16, side + 128 : side + 256] = tile
        for side in (0, 256):
            fields[shift, :, side : side + 256] = jnp.dot(
                mask_turned, slots[slot, :, side : side + 256], preferred_element_type=jnp.float32
            ).astype(jnp.bfloat16)

    for shift in range(shifts):
        one_shift(shift, shift % 4)


def lane_row(count, value):
    lane = lax.broadcasted_iota(jnp.int32, (1, lanes), 1)
    row = jnp.zeros((1, lanes), jnp.float32)
    for t in range(count):
        row = jnp.where(lane == t, value(t), row)
    return row


def plane_kernel(
    n, wide, mask_hbm, coords_hbm, weights_hbm, focus_hbm, taps_hbm, blur_x_hbm, blur_y_hbm,
    blur_z_hbm, intensity_ref, latent_ref, mask_ref, coords_ref, weights_ref, focus_ref, taps_ref,
    blur_x_ref, blur_y_ref, blur_z_ref, arg_sems, rows, t0, t1, t2, t3, slots, fields, shapes, image,
    acid, centre, mix, own, points, points_smem, along, columns, mixed, planes, send_sems, recv_sems,
    local_sem,
):
    me = lax.axis_index("src")
    group = lax.axis_index("groups")
    local = weights_ref.shape[0]
    tap_count, blur_count = taps_ref.shape[0], blur_x_ref.shape[0]
    barrier = pltpu.get_barrier_semaphore()

    def each(action):
        lax.fori_loop(1, n, lambda off, carry: (action(off), carry)[1], 0)

    def peer(off):
        return (group, lax.rem(me + off, n))

    def signal(off):
        pl.semaphore_signal(
            barrier, inc=1, device_id=peer(off), device_id_type=pl.DeviceIdType.MESH
        )

    def copy(phase, source, target, off, slot):
        return pltpu.make_async_remote_copy(
            src_ref=source(off),
            dst_ref=target.at[slot],
            send_sem=send_sems.at[phase],
            recv_sem=recv_sems.at[phase],
            device_id=peer(off),
            device_id_type=pl.DeviceIdType.MESH,
        )

    def start(phase, source, target):
        each(lambda off: copy(phase, source, target, off, me).start())

    def whole(phase, target):
        others = target.at[pl.ds(0, n - 1)]
        return pltpu.make_async_remote_copy(
            src_ref=others,
            dst_ref=others,
            send_sem=send_sems.at[phase],
            recv_sem=recv_sems.at[phase],
            device_id=peer(1),
            device_id_type=pl.DeviceIdType.MESH,
        )

    def receive(phase, target):
        whole(phase, target).wait_recv()

    def sent(phase, target):
        whole(phase, target).wait_send()

    def blocks(ref, part):
        return lambda off: ref.at[part, lax.rem(me + off, n)]

    fetches = [
        pltpu.make_async_copy(source, target, arg_sems.at[place])
        for place, (source, target) in enumerate(
            (
                (coords_hbm, coords_ref),
                (weights_hbm, weights_ref),
                (focus_hbm, focus_ref),
                (taps_hbm, taps_ref),
                (blur_x_hbm, blur_x_ref),
                (blur_y_hbm, blur_y_ref),
                (blur_z_hbm, blur_z_ref),
                (mask_hbm, mask_ref),
            )
        )
    ]
    for fetch in fetches:
        fetch.start()
    each(signal)
    for fetch in fetches[:2]:
        fetch.wait()
    lane = lax.broadcasted_iota(jnp.int32, (1, 128), 1)
    packed = jnp.zeros((1, 128), jnp.int32)
    for s in range(local):
        packed = jnp.where(lane == 3 * s, coords_ref[s, 0], packed)
        packed = jnp.where(lane == 3 * s + 1, coords_ref[s, 1], packed)
        packed = jnp.where(lane == 3 * s + 2, weights_ref[s], packed)
    own[...] = packed
    points[me] = packed
    point_source = lambda off: own

    def send_point():
        pl.semaphore_wait(barrier, n - 1)
        each(lambda off: copy(0, point_source, points, n - off, me).start())

    late = me >= n // 2
    pl.when(late)(send_point)
    slots[...] = jnp.zeros_like(slots)
    for fetch in fetches[2:]:
        fetch.wait()
    rows[0:1, :] = lane_row(tap_count, lambda t: taps_ref[t])
    rows[1:2, :] = lane_row(tap_count, lambda t: taps_ref[tap_count - 1 - t])
    rows[2:3, :] = lane_row(blur_count, lambda t: blur_x_ref[t] / blur_count)
    rows[3:4, :] = lane_row(blur_count, lambda t: blur_y_ref[blur_count - 1 - t] / blur_count)
    focus = focus_ref[me].astype(jnp.float32)
    store_taps(rows, 0, focus, 1.0, t0, t1, tap_count)
    store_taps(rows, 1, focus, -1.0, t2, t3, tap_count)
    pl.when(jnp.logical_not(late))(send_point)
    build_tables(t0, t1, t2, t3, mask_ref, slots, shapes, fields)
    image[...] = jnp.zeros_like(image)
    tiles = toeplitz_tiles(rows[2:3, :128], 15, range(-1, 9))
    blank = jnp.zeros((112, 128), jnp.float32)
    blur_low = jnp.concatenate(
        [
            jnp.concatenate([tiles[j] for j in range(8)], axis=0),
            jnp.concatenate([blank, tiles[-1]], axis=0)[:, :16],
        ],
        axis=1,
    )
    blur_high = jnp.concatenate(
        [
            jnp.concatenate([tiles[j] for j in range(1, 9)], axis=0),
            jnp.concatenate([blank[:96], tiles[-1], tiles[0]], axis=0)[:, :16],
        ],
        axis=1,
    )
    back_y = rows[3:4, :]
    store_toeplitz(rows[3:4, :128], 241, ((centre, 0, 0, 1),))
    tall = jnp.broadcast_to(back_y, (16, lanes))
    before = pltpu.roll(tall, lanes - 31, 1, stride=1, stride_axis=0)[:, :256]
    after = pltpu.roll(tall, 241, 1, stride=1, stride_axis=0)[:, :256]
    pad = jnp.zeros((112, 256), jnp.float32)
    size = n * wide
    distance = lax.broadcasted_iota(jnp.int32, (size, size), 0) - lax.broadcasted_iota(
        jnp.int32, (size, size), 1
    )
    mixing = jnp.zeros((size, size), jnp.float32)
    for lag in range(1 - n, n):
        mixing = jnp.where(distance == lag * wide, blur_z_ref[lag + n - 1] / n, mixing)
    mix[...] = mixing
    receive(0, points)
    to_smem = pltpu.make_async_copy(points, points_smem, local_sem)
    to_smem.start()
    to_smem.wait()

    def image_columns(left, low, high, first):
        count = high - low

        def some_devices(step, carry):
            power = jnp.zeros((count, 256), jnp.float32)
            for place in range(devices_unrolled * local):
                device, s = devices_unrolled * step + place // local, place % local
                point = [points_smem[device, 0, 3 * s + item] for item in range(3)]
                factor = point[2].astype(jnp.float32) / (4.0 * local * n)
                column, row = point[0] + max_shift, point[1] + max_shift
                field = jnp.dot(
                    jnp.concatenate(
                        [shapes[column, low:high], shapes[column, 128 + low : 128 + high]], axis=0
                    ),
                    jnp.concatenate(
                        [
                            fields[row, first : first + 128, :256],
                            fields[row, first : first + 128, 256:],
                        ],
                        axis=0,
                    ),
                    preferred_element_type=jnp.float32,
                )
                power = power + factor * (field[:count] ** 2 + field[count:] ** 2)
            image[left : left + count] += power
            return carry

        lax.fori_loop(0, n // devices_unrolled, some_devices, 0)
        acid[left : left + count] = 1.0 - jnp.exp(-dose_scale * image[left : left + count])

    def send_columns(part, values):
        along[part] = values.reshape(n, wide, 256)
        start(1 + part, blocks(along, part), columns.at[part])
        columns[part, me] = along[part, me]

    def mix_planes(part):
        receive(1 + part, columns.at[part])
        stack = columns[part].reshape(size, 256)
        zero = jnp.zeros((wide, 128), jnp.float32)
        along_y = (
            exact_dot(stack, centre[...])
            + exact_dot(
                jnp.concatenate([zero, stack[:-wide, 128:]], axis=0),
                jnp.concatenate([pad, before], axis=0),
            )
            + exact_dot(
                jnp.concatenate([stack[wide:, :128], zero], axis=0),
                jnp.concatenate([after, pad], axis=0),
            )
        )
        mixed[part] = exact_dot(mix[...], along_y).reshape(n, wide, 256)
        start(3 + part, blocks(mixed, part), planes.at[part])
        planes[part, me] = mixed[part, me]

    image_columns(0, 0, 96, 0)
    image_columns(96, 32, 96, 64)
    send_columns(0, exact_dot(blur_low, acid[:144]))
    image_columns(160, 32, 128, 128)
    send_columns(1, exact_dot(blur_high, acid[112:]))
    intensity_ref[...] = image[...].T
    mix_planes(0)
    mix_planes(1)
    sent(0, points)
    sent(1, columns.at[0])
    sent(2, columns.at[1])
    sent(3, planes.at[0])
    receive(3, planes.at[0])
    latent_ref[:, :size] = planes[0].reshape(size, 256).T
    sent(4, planes.at[1])
    receive(4, planes.at[1])
    latent_ref[:, size:] = planes[1].reshape(size, 256).T


def store_kernel(intensity_ref, latent_ref, intensity_hbm, latent_hbm, sems):
    stores = [
        pltpu.make_async_copy(intensity_ref, intensity_hbm, sems.at[0]),
        pltpu.make_async_copy(latent_ref, latent_hbm, sems.at[1]),
    ]
    for store in stores:
        store.start()
    for store in stores:
        store.wait()


def plane_per_device(
    layout_mask, source_coords, source_weights, focus_steps, pupil_taps, blur_x, blur_y, blur_z
):
    n = lax.axis_size("src")
    wide = layout_mask.shape[1] // n // 2
    square = jax.ShapeDtypeStruct((256, 256), jnp.float32)
    full = pltpu.VMEM((256, 256), jnp.float32)
    parts = pltpu.VMEM((2, n, wide, 256), jnp.float32)
    vmem = pl.BlockSpec(memory_space=pltpu.VMEM)
    hbm = pl.BlockSpec(memory_space=pltpu.HBM)
    arguments = (
        source_coords, source_weights, focus_steps, pupil_taps, blur_x, blur_y, blur_z
    )
    made = pl.pallas_call(
        lambda *refs: plane_kernel(n, wide, *refs),
        out_shape=(square, square),
        in_specs=[hbm] * 8,
        out_specs=(vmem, vmem),
        scratch_shapes=[pltpu.VMEM((256, 256), jnp.int32)]
        + [pltpu.SMEM(value.shape, value.dtype) for value in arguments]
        + [pltpu.SemaphoreType.DMA((8,)), pltpu.VMEM((8, lanes), jnp.float32)]
        + [pltpu.VMEM((24, 128), jnp.float32)] * 4
        + [
            pltpu.VMEM((4, 256, 512), jnp.bfloat16),
            pltpu.VMEM((shifts, 256, 512), jnp.bfloat16),
            pltpu.VMEM((shifts, 256, 256), jnp.bfloat16),
            full,
            full,
            full,
            pltpu.VMEM((n * wide, n * wide), jnp.float32),
            pltpu.VMEM((1, 128), jnp.int32),
            pltpu.VMEM((n, 1, 128), jnp.int32),
            pltpu.SMEM((n, 1, 128), jnp.int32),
            parts,
            parts,
            parts,
            parts,
            pltpu.SemaphoreType.DMA((5,)),
            pltpu.SemaphoreType.DMA((5,)),
            pltpu.SemaphoreType.DMA,
        ],
        compiler_params=pltpu.CompilerParams(
            vmem_limit_bytes=32 * 2**20, collective_id=0, has_side_effects=True
        ),
    )(*[pltpu.with_memory_space_constraint(value, pltpu.HBM) for value in (layout_mask, *arguments)])
    return pl.pallas_call(
        store_kernel,
        out_shape=(square, square),
        in_specs=[vmem] * 2,
        out_specs=(hbm, hbm),
        scratch_shapes=[pltpu.SemaphoreType.DMA((2,))],
    )(*[pltpu.with_memory_space_constraint(value, pltpu.VMEM) for value in made])


def solution(mesh):
    in_specs = (P("groups", None), P("src", None), P("src"), P(), P(), P(), P(), P())
    out_specs = (P(("groups", "src"), None), P(("groups", "src"), None))
    body = plane_per_device if mesh.shape["src"] == 16 else on_device
    return jax.shard_map(
        body, mesh=mesh, in_specs=in_specs, out_specs=out_specs, check_vma=False
    )
```

```python
import math

import jax
import jax.numpy as jnp
from jax import lax
from jax.experimental import pallas as pl
from jax.experimental.pallas import tpu as pltpu
from jax.sharding import PartitionSpec as P

two_pi = 2.0 * math.pi
defocus_scale = 0.8
dose_scale = 2.0


def extended_2(block, sides, width):
    for axis, dim in sides:
        count = lax.axis_size(axis)
        forward = [(i, i + 1) for i in range(count - 1)]
        backward = [(target, source) for source, target in forward]
        low = lax.ppermute(
            lax.slice_in_dim(block, block.shape[dim] - width, None, axis=dim), axis, forward
        )
        high = lax.ppermute(lax.slice_in_dim(block, 0, width, axis=dim), axis, backward)
        block = jnp.concatenate([low, block, high], axis=dim)
    return block


def passed_along(block, axis, distance):
    devices = range(lax.axis_size(axis))
    route = [(i - distance, i) for i in devices if i - distance in devices]
    return lax.ppermute(block, axis, route)


def tap_matrix(out_pos, extent, tilt_index, focus_step, pupil_taps):
    tap_count = pupil_taps.shape[0]
    centre = (tap_count - 1) / 2.0
    column_pos = jnp.arange(extent, dtype=jnp.int32)
    offset = column_pos[None, :] - out_pos[:, None] + tap_count // 2
    inside = (offset >= 0) & (offset < tap_count)
    clipped = jnp.clip(offset, 0, tap_count - 1)
    amplitude = jnp.take(pupil_taps, clipped) / math.sqrt(tap_count)
    relative = clipped.astype(jnp.float32) - centre
    phase_angle = (
        two_pi * tilt_index.astype(jnp.float32) * relative / tap_count
        + defocus_scale * focus_step.astype(jnp.float32) * (relative / centre) ** 2
    )
    real_part = jnp.where(inside, amplitude * jnp.cos(phase_angle), jnp.zeros_like(amplitude))
    imag_part = jnp.where(inside, amplitude * jnp.sin(phase_angle), jnp.zeros_like(amplitude))
    return (real_part.astype(jnp.bfloat16), imag_part.astype(jnp.bfloat16))


def field_power(mask_bf, row_pos, tilt_x, tilt_y, focus_step, pupil_taps):
    rows_tile, cols_tile = mask_bf.shape
    row_count = row_pos.shape[0]
    col_pos = jnp.arange(cols_tile, dtype=jnp.int32)
    rows_real, rows_imag = tap_matrix(row_pos, rows_tile, tilt_y, focus_step, pupil_taps)
    cols_real, cols_imag = tap_matrix(col_pos, cols_tile, tilt_x, focus_step, pupil_taps)
    stacked = jnp.concatenate([rows_real, rows_imag], axis=0)
    first_pass = jnp.dot(stacked, mask_bf, preferred_element_type=jnp.float32).astype(jnp.bfloat16)
    joined = jnp.concatenate([first_pass[:row_count], first_pass[row_count:]], axis=1)
    upper_half = jnp.concatenate([cols_real.T, cols_imag.T], axis=1)
    lower_half = jnp.concatenate([-cols_imag.T, cols_real.T], axis=1)
    pupil_cols = jnp.concatenate([upper_half, lower_half], axis=0)
    field_parts = jnp.dot(joined, pupil_cols, preferred_element_type=jnp.float32)
    return field_parts[:, :cols_tile] ** 2 + field_parts[:, cols_tile:] ** 2


def on_device(
    layout_mask, source_coords, source_weights, focus_steps, pupil_taps, blur_x, blur_y, blur_z
):
    rows_tile, cols_tile = layout_mask.shape
    planes = focus_steps.shape[0]
    devices = lax.axis_size("src")
    src_local = source_coords.shape[0]
    mask_bf = layout_mask.astype(jnp.bfloat16)
    own_rows = planes * rows_tile // devices
    per_plane = devices // planes
    factors = source_weights.astype(jnp.float32) / (4.0 * src_local * devices)
    row_pos = jnp.arange(rows_tile, dtype=jnp.int32)

    def plane_term(focus_step):
        running = jnp.zeros((rows_tile, cols_tile), jnp.float32)
        for source in range(src_local):
            power = field_power(
                mask_bf,
                row_pos,
                source_coords[source, 0],
                source_coords[source, 1],
                focus_step,
                pupil_taps,
            )
            running = running + factors[source] * power
        return running

    partial_sum = lax.map(plane_term, focus_steps).reshape(planes * rows_tile, cols_tile)
    intensity = lax.psum_scatter(partial_sum, "src", scatter_dimension=0, tiled=True)
    acid_level = 1.0 - jnp.exp(-dose_scale * intensity)
    width_x = blur_x.shape[0]
    half_x = width_x // 2
    padded = jnp.pad(acid_level, ((0, 0), (half_x, half_x)))
    along_x = jnp.zeros_like(acid_level)
    for tap_index in range(width_x):
        along_x = (
            along_x + blur_x[tap_index] / width_x * padded[:, tap_index : tap_index + cols_tile]
        )
    width_y = blur_y.shape[0]
    half_y = width_y // 2
    extended = extended_2(along_x, (("src", 0),), half_y)
    along_y = jnp.zeros_like(along_x)
    for tap_index in range(width_y):
        along_y = along_y + blur_y[tap_index] / width_y * extended[tap_index : tap_index + own_rows]
    latent = blur_z[planes - 1] / planes * along_y
    for plane_lag in range(1 - planes, planes):
        if plane_lag != 0:
            arrived = passed_along(along_y, "src", plane_lag * per_plane)
            latent = latent + blur_z[plane_lag + planes - 1] / planes * arrived
    return (intensity, latent)


max_shift = 8
shifts = 2 * max_shift + 1
lanes = 512
devices_unrolled = 16


def halves(value):
    high = value.astype(jnp.bfloat16)
    return high, (value - high.astype(jnp.float32)).astype(jnp.bfloat16)


def exact_dot(left, right):
    def product(a, b):
        return jnp.dot(a, b, preferred_element_type=jnp.float32)

    left_high, left_low = left if isinstance(left, tuple) else halves(left)
    right_high, right_low = right if isinstance(right, tuple) else halves(right)
    return (
        product(left_high, right_low) + product(left_low, right_high)
    ) + product(left_high, right_high)


def store_toeplitz(row, position, pieces, apart=128):
    base = pltpu.roll(jnp.broadcast_to(row, (16, 128)), 0, 1, stride=1, stride_axis=0)
    lane = lax.broadcasted_iota(jnp.int32, (16, 128), 1)
    zero = jnp.zeros((16, 128), jnp.float32)
    for j in range(8):
        first = 16 * j + position - 256
        turn, tile = first % 128, first // 128
        rolled = pltpu.roll(base, turn, 1) if turn else base
        wraps = turn > 65
        kept = jnp.where(lane >= turn, rolled, zero) if wraps else rolled
        wrapped = jnp.where(lane < turn, rolled, zero) if wraps else zero
        for block, start in ((j, tile), (j + 8, tile + 1)):
            for column in range(2):
                part = kept if column == start else wrapped if column == start + 1 else zero
                for ref, top, side, sign in pieces:
                    value = part if sign > 0 else -part
                    left = side + apart * column
                    ref[top + 16 * block : top + 16 * block + 16, left : left + 128] = (
                        value.astype(ref.dtype)
                    )


def store_taps(taps_ref, row, focus, flip, real_ref, imag_ref, tap_count):
    centre = (tap_count - 1) / 2.0
    amplitude = taps_ref[row : row + 1, :128] / math.sqrt(tap_count)
    shape = (24, 128)
    relative = (lax.broadcasted_iota(jnp.int32, shape, 1).astype(jnp.float32) - centre) * flip
    tilt = (lax.broadcasted_iota(jnp.int32, shape, 0) - max_shift).astype(jnp.float32)
    phase = (
        two_pi * tilt * relative / tap_count + defocus_scale * focus * (relative / centre) ** 2
    )
    real_ref[...] = amplitude * jnp.cos(phase)
    imag_ref[...] = amplitude * jnp.sin(phase)


def toeplitz_tiles(row, position, blocks, dtype=jnp.float32):
    base = pltpu.roll(jnp.broadcast_to(row, (16, 128)), 0, 1, stride=1, stride_axis=0)
    apart = lax.broadcasted_iota(jnp.int32, (16, 128), 1) - lax.broadcasted_iota(
        jnp.int32, (16, 128), 0
    )
    base = base.astype(dtype)
    tiles = {}
    for block in blocks:
        turn = 16 * block - position
        tile = pltpu.roll(base, turn % 128, 1) if turn % 128 else base
        if 127 - turn >= 128:
            tile = jnp.where(apart < 128 + turn, tile, jnp.zeros_like(tile))
        if -15 - turn < -80:
            tile = jnp.where(apart >= turn - 80, tile, jnp.zeros_like(tile))
        tiles[block] = tile
    return tiles


def build_tables(forward_real, forward_imag, back_real, back_imag, mask_ref, slots, shapes, fields):
    mask_turned = mask_ref[...].astype(jnp.float32).T.astype(jnp.bfloat16)

    def one_shift(shift, slot):
        row = pl.ds(shift, 1)
        real = toeplitz_tiles(forward_real[row, :], 24, range(8), jnp.bfloat16)
        imag = toeplitz_tiles(forward_imag[row, :], 24, range(8), jnp.bfloat16)
        for j in range(8):
            upper, lower = slice(16 * j, 16 * j + 16), slice(128 + 16 * j, 144 + 16 * j)
            shapes[shift, upper, :128] = real[j]
            shapes[shift, upper, 128:] = -imag[j]
            shapes[shift, lower, :128] = imag[j]
            shapes[shift, lower, 128:] = real[j]
        for side, source in ((0, back_real), (256, back_imag)):
            tiles = toeplitz_tiles(source[row, :], 23, range(-2, 10), jnp.bfloat16)
            for block, tile in tiles.items():
                if block >= 0:
                    slots[slot, 16 * block : 16 * block + 16, side : side + 128] = tile
                if block < 8:
                    top = 16 * block + 128
                    slots[slot, top : top + 16, side + 128 : side + 256] = tile
        for side in (0, 256):
            fields[shift, :, side : side + 256] = jnp.dot(
                mask_turned, slots[slot, :, side : side + 256], preferred_element_type=jnp.float32
            ).astype(jnp.bfloat16)

    for shift in range(shifts):
        one_shift(shift, shift % 4)


def lane_row(count, value):
    lane = lax.broadcasted_iota(jnp.int32, (1, lanes), 1)
    row = jnp.zeros((1, lanes), jnp.float32)
    for t in range(count):
        row = jnp.where(lane == t, value(t), row)
    return row


def plane_kernel(
    n, wide, mask_hbm, coords_hbm, weights_hbm, focus_hbm, taps_hbm, blur_x_hbm, blur_y_hbm,
    blur_z_hbm, intensity_ref, latent_ref, mask_ref, coords_ref, weights_ref, focus_ref, taps_ref,
    blur_x_ref, blur_y_ref, blur_z_ref, arg_sems, rows, t0, t1, t2, t3, slots, fields, shapes, image,
    acid, centre, centre_parts, edge_parts, mix_parts, own, points, points_smem, along, columns, mixed, planes, send_sems, recv_sems,
):
    me = lax.axis_index("src")
    group = lax.axis_index("groups")
    local = weights_ref.shape[0]
    tap_count, blur_count = taps_ref.shape[0], blur_x_ref.shape[0]
    barrier = pltpu.get_barrier_semaphore()

    def each(action):
        lax.fori_loop(1, n, lambda off, carry: (action(off), carry)[1], 0)

    def peer(off):
        return (group, lax.rem(me + off, n))

    def signal(off):
        pl.semaphore_signal(
            barrier, inc=1, device_id=peer(off), device_id_type=pl.DeviceIdType.MESH
        )

    def copy(phase, source, target, off, slot):
        return pltpu.make_async_remote_copy(
            src_ref=source(off),
            dst_ref=target.at[slot],
            send_sem=send_sems.at[phase],
            recv_sem=recv_sems.at[phase],
            device_id=peer(off),
            device_id_type=pl.DeviceIdType.MESH,
        )

    def start(phase, source, target):
        each(lambda off: copy(phase, source, target, off, me).start())

    def whole(phase, target):
        others = target.at[pl.ds(0, n - 1)]
        return pltpu.make_async_remote_copy(
            src_ref=others,
            dst_ref=others,
            send_sem=send_sems.at[phase],
            recv_sem=recv_sems.at[phase],
            device_id=peer(1),
            device_id_type=pl.DeviceIdType.MESH,
        )

    def receive(phase, target):
        whole(phase, target).wait_recv()

    def sent(phase, target):
        whole(phase, target).wait_send()

    def blocks(ref, part):
        return lambda off: ref.at[part, lax.rem(me + off, n)]

    fetches = [
        pltpu.make_async_copy(source, target, arg_sems.at[place])
        for place, (source, target) in enumerate(
            (
                (coords_hbm, coords_ref),
                (weights_hbm, weights_ref),
                (focus_hbm, focus_ref),
                (taps_hbm, taps_ref),
                (blur_x_hbm, blur_x_ref),
                (blur_y_hbm, blur_y_ref),
                (blur_z_hbm, blur_z_ref),
                (mask_hbm, mask_ref),
            )
        )
    ]
    for fetch in fetches:
        fetch.start()
    each(signal)
    for fetch in fetches[:2]:
        fetch.wait()
    lane = lax.broadcasted_iota(jnp.int32, (1, 128), 1)
    packed = jnp.zeros((1, 128), jnp.int32)
    for s in range(local):
        packed = jnp.where(lane == 3 * s, coords_ref[s, 0], packed)
        packed = jnp.where(lane == 3 * s + 1, coords_ref[s, 1], packed)
        packed = jnp.where(lane == 3 * s + 2, weights_ref[s], packed)
    own[...] = packed
    points[me] = packed
    point_source = lambda off: own

    def send_point():
        pl.semaphore_wait(barrier, n - 1)
        each(lambda off: copy(0, point_source, points, n - off, me).start())

    late = me >= n // 2
    pl.when(late)(send_point)
    slots[...] = jnp.zeros_like(slots)
    for fetch in fetches[2:]:
        fetch.wait()
    rows[0:1, :] = lane_row(tap_count, lambda t: taps_ref[t])
    rows[1:2, :] = lane_row(tap_count, lambda t: taps_ref[tap_count - 1 - t])
    rows[2:3, :] = lane_row(blur_count, lambda t: blur_x_ref[t] / blur_count)
    rows[3:4, :] = lane_row(blur_count, lambda t: blur_y_ref[blur_count - 1 - t] / blur_count)
    focus = focus_ref[me].astype(jnp.float32)
    store_taps(rows, 0, focus, 1.0, t0, t1, tap_count)
    store_taps(rows, 1, focus, -1.0, t2, t3, tap_count)
    pl.when(jnp.logical_not(late))(send_point)
    build_tables(t0, t1, t2, t3, mask_ref, slots, shapes, fields)
    image[...] = jnp.zeros_like(image)
    tiles = toeplitz_tiles(rows[2:3, :128], 15, range(-1, 9))
    blank = jnp.zeros((112, 128), jnp.float32)
    blur_low = jnp.concatenate(
        [
            jnp.concatenate([tiles[j] for j in range(8)], axis=0),
            jnp.concatenate([blank, tiles[-1]], axis=0)[:, :16],
        ],
        axis=1,
    )
    blur_high = jnp.concatenate(
        [
            jnp.concatenate([tiles[j] for j in range(1, 9)], axis=0),
            jnp.concatenate([blank[:96], tiles[-1], tiles[0]], axis=0)[:, :16],
        ],
        axis=1,
    )
    back_y = rows[3:4, :]
    store_toeplitz(rows[3:4, :128], 241, ((centre, 0, 0, 1),))
    tall = jnp.broadcast_to(back_y, (16, lanes))
    before = pltpu.roll(tall, lanes - 31, 1, stride=1, stride_axis=0)[:, :256]
    after = pltpu.roll(tall, 241, 1, stride=1, stride_axis=0)[:, :256]
    pad = jnp.zeros((112, 256), jnp.float32)
    size = n * wide
    distance = lax.broadcasted_iota(jnp.int32, (size, size), 0) - lax.broadcasted_iota(
        jnp.int32, (size, size), 1
    )
    mixing = jnp.zeros((size, size), jnp.float32)
    for lag in range(1 - n, n):
        mixing = jnp.where(distance == lag * wide, blur_z_ref[lag + n - 1] / n, mixing)
    for ref, value in (
        (centre_parts, centre[...]),
        (edge_parts, jnp.concatenate([after, pad, pad, before], axis=0)),
        (mix_parts, mixing),
    ):
        ref[0], ref[1] = halves(value)
    receive(0, points)
    for device in range(n):
        row = points[device]
        for item in range(3 * local):
            points_smem[device, 0, item] = row[0, item]

    def image_columns(left, low, high, first):
        count = high - low

        def some_devices(step, carry):
            power = jnp.zeros((count, 256), jnp.float32)
            for place in range(devices_unrolled * local):
                device, s = devices_unrolled * step + place // local, place % local
                point = [points_smem[device, 0, 3 * s + item] for item in range(3)]
                factor = point[2].astype(jnp.float32) / (4.0 * local * n)
                column, row = point[0] + max_shift, point[1] + max_shift
                field = jnp.dot(
                    jnp.concatenate(
                        [shapes[column, low:high], shapes[column, 128 + low : 128 + high]], axis=0
                    ),
                    jnp.concatenate(
                        [
                            fields[row, first : first + 128, :256],
                            fields[row, first : first + 128, 256:],
                        ],
                        axis=0,
                    ),
                    preferred_element_type=jnp.float32,
                )
                power = power + factor * (field[:count] ** 2 + field[count:] ** 2)
            image[left : left + count] += power
            return carry

        lax.fori_loop(0, n // devices_unrolled, some_devices, 0)
        acid[left : left + count] = 1.0 - jnp.exp(-dose_scale * image[left : left + count])

    def send_columns(part, values):
        along[part] = values.reshape(n, wide, 256)
        start(1 + part, blocks(along, part), columns.at[part])
        columns[part, me] = along[part, me]

    def mix_planes(part):
        receive(1 + part, columns.at[part])
        stack = columns[part].reshape(size, 256)
        zero = jnp.zeros((wide, 128), jnp.float32)
        along_y = exact_dot(stack, (centre_parts[0], centre_parts[1])) + exact_dot(
            jnp.concatenate(
                [
                    jnp.concatenate([stack[wide:, :128], zero], axis=0),
                    jnp.concatenate([zero, stack[:-wide, 128:]], axis=0),
                ],
                axis=1,
            ),
            (edge_parts[0], edge_parts[1]),
        )
        mixed[part] = exact_dot((mix_parts[0], mix_parts[1]), along_y).reshape(n, wide, 256)
        start(3 + part, blocks(mixed, part), planes.at[part])
        planes[part, me] = mixed[part, me]

    image_columns(0, 0, 96, 0)
    image_columns(96, 32, 96, 64)
    send_columns(0, exact_dot(blur_low, acid[:144]))
    image_columns(160, 32, 128, 128)
    send_columns(1, exact_dot(blur_high, acid[112:]))
    mix_planes(0)
    mix_planes(1)
    intensity_ref[...] = image[...].T
    sent(0, points)
    sent(1, columns.at[0])
    sent(2, columns.at[1])
    sent(3, planes.at[0])
    receive(3, planes.at[0])
    latent_ref[:, :size] = planes[0].reshape(size, 256).T
    sent(4, planes.at[1])
    receive(4, planes.at[1])
    latent_ref[:, size:] = planes[1].reshape(size, 256).T


def store_kernel(intensity_ref, latent_ref, intensity_hbm, latent_hbm, sems):
    stores = [
        pltpu.make_async_copy(intensity_ref, intensity_hbm, sems.at[0]),
        pltpu.make_async_copy(latent_ref, latent_hbm, sems.at[1]),
    ]
    for store in stores:
        store.start()
    for store in stores:
        store.wait()


def plane_per_device(
    layout_mask, source_coords, source_weights, focus_steps, pupil_taps, blur_x, blur_y, blur_z
):
    n = lax.axis_size("src")
    wide = layout_mask.shape[1] // n // 2
    square = jax.ShapeDtypeStruct((256, 256), jnp.float32)
    full = pltpu.VMEM((256, 256), jnp.float32)
    parts = pltpu.VMEM((2, n, wide, 256), jnp.float32)
    vmem = pl.BlockSpec(memory_space=pltpu.VMEM)
    hbm = pl.BlockSpec(memory_space=pltpu.HBM)
    arguments = (
        source_coords, source_weights, focus_steps, pupil_taps, blur_x, blur_y, blur_z
    )
    made = pl.pallas_call(
        lambda *refs: plane_kernel(n, wide, *refs),
        out_shape=(square, square),
        in_specs=[hbm] * 8,
        out_specs=(vmem, vmem),
        scratch_shapes=[pltpu.VMEM((256, 256), jnp.int32)]
        + [pltpu.SMEM(value.shape, value.dtype) for value in arguments]
        + [pltpu.SemaphoreType.DMA((8,)), pltpu.VMEM((8, lanes), jnp.float32)]
        + [pltpu.VMEM((24, 128), jnp.float32)] * 4
        + [
            pltpu.VMEM((4, 256, 512), jnp.bfloat16),
            pltpu.VMEM((shifts, 256, 512), jnp.bfloat16),
            pltpu.VMEM((shifts, 256, 256), jnp.bfloat16),
            full,
            full,
            full,
            pltpu.VMEM((2, 256, 256), jnp.bfloat16),
            pltpu.VMEM((2, 256, 256), jnp.bfloat16),
            pltpu.VMEM((2, n * wide, n * wide), jnp.bfloat16),
            pltpu.VMEM((1, 128), jnp.int32),
            pltpu.VMEM((n, 1, 128), jnp.int32),
            pltpu.SMEM((n, 1, 128), jnp.int32),
            parts,
            parts,
            parts,
            parts,
            pltpu.SemaphoreType.DMA((5,)),
            pltpu.SemaphoreType.DMA((5,)),
        ],
        compiler_params=pltpu.CompilerParams(
            vmem_limit_bytes=32 * 2**20, collective_id=0, has_side_effects=True
        ),
    )(*[pltpu.with_memory_space_constraint(value, pltpu.HBM) for value in (layout_mask, *arguments)])
    return pl.pallas_call(
        store_kernel,
        out_shape=(square, square),
        in_specs=[vmem] * 2,
        out_specs=(hbm, hbm),
        scratch_shapes=[pltpu.SemaphoreType.DMA((2,))],
    )(*[pltpu.with_memory_space_constraint(value, pltpu.VMEM) for value in made])


def solution(mesh):
    in_specs = (P("groups", None), P("src", None), P("src"), P(), P(), P(), P(), P())
    out_specs = (P(("groups", "src"), None), P(("groups", "src"), None))
    body = plane_per_device if mesh.shape["src"] == 16 else on_device
    return jax.shard_map(
        body, mesh=mesh, in_specs=in_specs, out_specs=out_specs, check_vma=False
    )
```
